256 devices in a mesh: role: 4 (over y), batch: 8 (over z_hi, core), tensor: 8 (over z_lo, x).
Axes of the slice: x: 4, y: 4, z: 8 (z_hi: 4, z_lo: 2; z = z_hi * 2 + z_lo), core: 2. Of those that a mesh axis runs over, the one named last changes fastest.
Arguments:
- span: bfloat16 [8192, 5120], P('batch', ('role', 'tensor')), may hold values from -6 to 6
- key_value_weight: bfloat16 [5120, 8, 256], P('role', 'tensor'), may hold values from -0.078125 to 0.078125
- queries: bfloat16 [3, 128, 64, 128], P(None, 'batch', 'tensor'), may hold values from -6 to 6
- cache_codes: bfloat16 [3, 128, 8, 256, 256], P(None, 'batch', 'tensor'), may hold values from -127 to 127
- cache_scales: float32 [3, 128, 8, 16, 2], P(None, 'batch', 'tensor'), may hold values from 0.005 to 0.05
- cache_len: int32 [3, 128], P(None, 'batch'), may hold values from 2 to 256
- block_dest: int32 [512, 1], replicated, may hold values from 0 to 23; in each aligned block of 64 rows (0 to 63, 64 to 127, ...) at most 5 rows name the same one
- block_row: int32 [512], replicated, may hold values from 0 to 15
Outputs:
- judged: bfloat16 [3, 128, 8192], P(None, 'batch', 'tensor')
The draws below stay inside these ranges and needn't reach their ends.
Inputs may be any that keep to these rules, and one draw needn't show every extreme that they name: `block_dest`: within the 64 blocks of each batch index's prompt (aligned blocks of rows), no value is named more than 5 times.
All inputs are finite; a program needn't handle non-finite values.
Results may differ from the reference program's by a relative error of at most 0.025.
Values may be sent and summed in bfloat16 or wider, within the bound.
No kernel may reach another device: no remote copies, remote signals or barrier semaphores. Data moves between devices by JAX's collectives and lax.ppermute only.
A program may use at most 64 MiB of HBM per device.

```python
import math
import jax
import jax.numpy as jnp
import numpy as np
from jax import lax

MODEL_WIDTH = 5120
QUERY_HEADS = 64
KEY_VALUE_HEADS = 8
HEAD_SIZE = 128
BLOCK_TOKENS = 16
RD = 16
CACHE_SLOTS = 256
DECODE_GROUPS = 3
DECODE_ROWS = 128
SPAN = 8192
NB = 64
BLOCKS = 512
DESTS = 24
CAP = 5
N_BATCH = 8


def draw_queries(key, part):
    key = jax.random.fold_in(key, 11)
    values = jnp.clip(jax.random.normal(key, (DECODE_GROUPS, DECODE_ROWS, QUERY_HEADS, HEAD_SIZE), jnp.float32), -6.0, 6.0)
    return values.astype(jnp.bfloat16)


def draw_cache_codes(key, part):
    key = jax.random.fold_in(key, 13)
    array_shape = (DECODE_GROUPS, DECODE_ROWS, KEY_VALUE_HEADS, CACHE_SLOTS, 2 * HEAD_SIZE)
    values = jnp.clip(40.0 * jax.random.normal(key, array_shape, jnp.float32), -127.0, 127.0)
    return values.astype(jnp.bfloat16)


def draw_cache_scales(key, part):
    key = jax.random.fold_in(key, 17)
    array_shape = (DECODE_GROUPS, DECODE_ROWS, KEY_VALUE_HEADS, CACHE_SLOTS // BLOCK_TOKENS, 2)
    lower = jnp.log(jnp.float32(0.005))
    upper = jnp.log(jnp.float32(0.05))
    values = jnp.exp(jax.random.uniform(key, array_shape, jnp.float32, lower, upper))
    values = jnp.clip(values, 0.005, 0.05)
    return values.astype(jnp.float32)


def draw_cache_len(key, part):
    key = jax.random.fold_in(key, 7)
    lengths = jax.random.randint(key, (DECODE_GROUPS, DECODE_ROWS), 2, CACHE_SLOTS + 1)
    return lengths.at[0, 0].set(CACHE_SLOTS).astype(jnp.int32)


def with_ends(values, stream_key, least, high):
    shape = values.shape
    spot = [jax.random.randint(jax.random.fold_in(stream_key, axis), (), 0, shape[axis]) for axis in range(len(shape))]
    values = values.at[tuple(spot)].set(least)
    longest = shape.index(max(shape))
    spot[longest] = (spot[longest] + 1) % shape[longest]
    return values.at[tuple(spot)].set(high)


def shard_levels(own_key, dims, shards, low, top_value):
    def one(dim, blocks):
        heights = jax.random.uniform(jax.random.fold_in(jax.random.fold_in(own_key, 6), dim), (blocks,), jnp.float32, low / len(shards), top_value / len(shards))
        return jnp.repeat(jnp.exp(heights), dims[dim] // blocks).reshape((-1,) + (1,) * (len(dims) - dim - 1))

    factor_of = one(*shards[0])
    for cut in shards[1:]:
        factor_of = factor_of * one(*cut)
    return factor_of


def deal_out(stream_key, own, number, rows, amount, top, most, lean):
    sequence = jax.random.permutation(stream_key, amount)
    packed, ordinary = portions_of(amount, rows * top, most, lean, True), portions_of(amount, rows * top, most, lean, False)
    places = jnp.arange(amount)

    def named(sizes, offset_by):
        used = int((sizes > 0).sum())
        fixed = max(1, used // 4)
        shifted = fixed + (places - fixed + offset_by * (used - fixed)) % max(1, amount - fixed)
        return jnp.zeros((amount,), jnp.int32).at[sequence[jnp.where(places < fixed, places, shifted)]].set(jnp.asarray(sizes, jnp.int32))

    sizes = jnp.where(number % 4 == 0, named(packed, number // 4), named(ordinary, number - number // 4 - 1))
    mixed = jax.random.permutation(jax.random.fold_in(own, 3), amount)
    donor, receiver = mixed[0:amount // 2 * 2:2], mixed[1:amount // 2 * 2:2]
    margin = jnp.minimum(sizes[donor] - 1, most - sizes[receiver]) // 2
    margin = jnp.where((donor == sequence[0]) | (receiver == sequence[0]) | (sizes[receiver] == 0), 0, jnp.maximum(margin, 0))
    shifted = jax.random.randint(jax.random.fold_in(own, 4), (amount // 2,), 0, 1 << 20) % (margin + 1)
    sizes = sizes.at[donor].add(-shifted).at[receiver].add(shifted)
    members = jnp.searchsorted(jnp.cumsum(sizes), jnp.arange(rows * top), side="right").astype(jnp.int32)
    grid = members.reshape(top, rows).T
    grid = grid[jax.random.permutation(jax.random.fold_in(own, 1), rows)]
    offset_by = jax.random.randint(jax.random.fold_in(own, 2), (rows, 1), 0, top)
    return jnp.take_along_axis(grid, (jnp.arange(top)[None, :] + offset_by) % top, axis=1)


def portions_of(number_of, total, limit, skew, full):
    loads = [(1 << 20) // math.isqrt(standing ** skew) + 1 for standing in range(1, number_of + 1)]
    largest = limit if full else min(limit, max(-(-total // number_of), total * loads[0] // sum(loads)))
    least = 1 if total - largest >= number_of - 1 else 0
    holding, rest = [largest] + [least] * (number_of - 1), total - largest - least * (number_of - 1)
    while rest > 0:
        candidates = [i for i in range(1, number_of) if holding[i] < largest] or [i for i in range(1, number_of) if holding[i] < limit]
        pool, remaining = sum([loads[i] for i in candidates]), rest
        for i in candidates:
            addition = min(limit - holding[i], max(1, remaining * loads[i] // pool), rest)
            holding[i] = holding[i] + addition
            rest = rest - addition
    return np.array(holding)


def bell_draw(own_key, extent, scale, reach, pieces=(), dtype=jnp.bfloat16):
    values = jax.random.normal(own_key, extent, jnp.float32) * scale
    if len(pieces) > 0:
        values = shard_levels(own_key, extent, pieces, -0.22, 0.18) * values
    return jnp.clip(values, min=-reach, max=reach).astype(dtype)


def setup_inputs(seed: int = 0) -> dict:
    key_of = jax.random.split(jax.random.key(seed), 9)
    span = bell_draw(key_of[0], (SPAN, MODEL_WIDTH), 1.0, 6.0, ((0, 8), (1, 32)))
    key_value_weight = bell_draw(key_of[1], (MODEL_WIDTH, KEY_VALUE_HEADS, 2 * HEAD_SIZE), MODEL_WIDTH ** -0.5, 0.078125, ((0, 4), (1, 8)))
    queries = draw_queries(jax.random.fold_in(key_of[8], 71), 0)
    cache_codes = draw_cache_codes(jax.random.fold_in(key_of[8], 71), 0)
    cache_scales = draw_cache_scales(jax.random.fold_in(key_of[8], 71), 0)
    cache_len = draw_cache_len(jax.random.fold_in(key_of[8], 71), 0)
    block_dest_keys = jax.random.split(jax.random.fold_in(key_of[6], 1), BLOCKS // NB)
    block_dest_turns = jax.random.permutation(jax.random.fold_in(key_of[6], 3), BLOCKS // NB)
    block_dest = jax.vmap(lambda own, number: deal_out(jax.random.fold_in(key_of[6], 2), own, number, NB, DESTS, 1, CAP, 2))(block_dest_keys, block_dest_turns).reshape((BLOCKS, 1))
    block_row = with_ends(jax.random.randint(key_of[7], (BLOCKS,), 0, RD), jax.random.fold_in(key_of[7], 1), 0, RD - 1).astype(jnp.int32)
    return dict(span=span, key_value_weight=key_value_weight, queries=queries, cache_codes=cache_codes, cache_scales=cache_scales, cache_len=cache_len, block_dest=block_dest, block_row=block_row)


def block_quantize(kv, heads, head_size, block):
    tokens = kv.shape[0]
    shaped = kv.reshape(tokens // block, block, heads, 2, head_size)
    largest = jnp.max(jnp.abs(shaped), axis=(1, 4))
    block_scales = (largest + 1e-6) / 127.0
    integer_codes = (shaped / block_scales[:, None, :, :, None]).astype(jnp.bfloat16)
    integer_codes = jnp.transpose(integer_codes, (0, 2, 1, 3, 4)).reshape(tokens // block, heads, block, 2 * head_size)
    return integer_codes, block_scales


def attend(query, res_codes, res_scales, length, new_codes, new_scales, target, block):
    rows, qheads, head_size = query.shape
    kv_heads = res_codes.shape[1]
    slots = res_codes.shape[2]
    grouped = query.reshape(rows, kv_heads, qheads // kv_heads, head_size)
    inverse = head_size ** -0.5
    key_scale = jnp.repeat(res_scales[..., 0], block, axis=2)
    value_scale = jnp.repeat(res_scales[..., 1], block, axis=2)
    resident = jnp.einsum("rhgd,rhpd->rhgp", grouped, res_codes[..., :head_size], preferred_element_type=jnp.float32)
    resident = resident * (key_scale * inverse)[:, :, None, :]
    live = jnp.arange(slots)[None, :] < length[:, None]
    resident = jnp.where(live[:, None, None, :], resident, -jnp.inf)
    fresh = jnp.einsum("rhgd,shtd->rhgst", grouped, new_codes[..., :head_size], preferred_element_type=jnp.float32)
    fresh = fresh * (new_scales[..., 0].T * inverse)[None, :, None, :, None]
    joined = target[None, :] == jnp.arange(rows)[:, None]
    fresh = jnp.where(joined[:, None, None, :, None], fresh, -jnp.inf)
    top = jnp.maximum(jnp.max(resident, axis=-1), jnp.max(fresh, axis=(-2, -1)))
    exp_res = jnp.exp(resident - top[..., None])
    exp_new = jnp.exp(fresh - top[..., None, None])
    total = jnp.sum(exp_res, axis=-1) + jnp.sum(exp_new, axis=(-2, -1))
    weight_res = (exp_res * value_scale[:, :, None, :]).astype(jnp.bfloat16)
    weight_new = (exp_new * new_scales[..., 1].T[None, :, None, :, None]).astype(jnp.bfloat16)
    summed = jnp.einsum("rhgp,rhpd->rhgd", weight_res, res_codes[..., head_size:], preferred_element_type=jnp.float32)
    summed = summed + jnp.einsum("rhgst,shtd->rhgd", weight_new, new_codes[..., head_size:], preferred_element_type=jnp.float32)
    return (summed / total[..., None]).reshape(rows, qheads * head_size).astype(jnp.bfloat16)


def reference(span, key_value_weight, queries, cache_codes, cache_scales, cache_len, block_dest, block_row):
    projected_rows = jnp.dot(span, key_value_weight.reshape(MODEL_WIDTH, KEY_VALUE_HEADS * 2 * HEAD_SIZE), preferred_element_type=jnp.float32)
    integer_codes, block_scales = block_quantize(projected_rows, KEY_VALUE_HEADS, HEAD_SIZE, BLOCK_TOKENS)
    dest = block_dest[:, 0]

    def one_group(group):
        target = jnp.where(dest // N_BATCH == group, (dest % N_BATCH) * RD + block_row, -1).astype(jnp.int32)
        return attend(queries[group], cache_codes[group], cache_scales[group], cache_len[group], integer_codes, block_scales, target, BLOCK_TOKENS)

    return lax.map(one_group, jnp.arange(DECODE_GROUPS).astype(jnp.int32))
```

```python
import jax
import jax.numpy as jnp
from jax import lax
from jax.experimental import pallas as pl
from jax.experimental.pallas import tpu as pltpu
from jax.sharding import PartitionSpec as P

BLOCK = 16
LOW = -1e38
F32 = jnp.float32
BF16 = jnp.bfloat16
VMEM = pl.BlockSpec(memory_space=pltpu.VMEM)
SMEM = pl.BlockSpec(memory_space=pltpu.SMEM)


def call(kernel, outs, args, specs, scratch=(), flops=0, nbytes=0):
    return pl.pallas_call(
        kernel,
        out_shape=outs,
        in_specs=specs,
        out_specs=jax.tree.map(lambda _: VMEM, outs),
        scratch_shapes=list(scratch),
        compiler_params=pltpu.CompilerParams(vmem_limit_bytes=40 * 1024 * 1024),
        cost_estimate=pl.CostEstimate(flops=flops, bytes_accessed=nbytes, transcendentals=0),
    )(*args)


def dot(a, b, ca, cb):
    return lax.dot_general(a, b, (((ca,), (cb,)), ((), ())), preferred_element_type=F32)


def three(v):
    hi = v.astype(BF16).astype(F32)
    mid = (v - hi).astype(BF16).astype(F32)
    return hi, mid, v - hi - mid


def cut_kernel(role_ref, x_ref, *outs):
    role = role_ref[0]
    tokens = x_ref.shape[0] // 4
    feats = x_ref.shape[1]
    for d in range(4):
        quarter = lax.rem(role + d, 4)
        rows = x_ref[pl.ds(pl.multiple_of(quarter * tokens, tokens), tokens), :].astype(F32)
        rows = jnp.concatenate([rows, jnp.zeros((tokens, 256 - feats), F32)], axis=1)
        outs[d][...] = jnp.transpose(rows)[:feats].astype(BF16)


def weight_kernel(slot_ref, core_ref, w_ref, own_ref, oth_ref, tmp):
    rows = w_ref.shape[0] // 8
    for s in range(8):
        start = pl.multiple_of(slot_ref[s] * rows, rows)
        tmp[pl.ds(s * rows, rows), :] = w_ref[pl.ds(start, rows), :].astype(F32)
    first = core_ref[0] == 0
    keys = jnp.transpose(tmp[:, :128]).astype(BF16)
    values = jnp.transpose(tmp[:, 128:]).astype(BF16)
    own_ref[...] = jnp.where(first, keys, values)
    oth_ref[...] = jnp.where(first, values, keys)


def pick_kernel(code_ref, q_ref, own_ref, oth_ref):
    q = q_ref[...]
    row = lax.broadcasted_iota(jnp.int32, (q.shape[0], 128), 0)
    for d in range(8):
        sel = jnp.where(row == code_ref[d : d + 1, :], 1.0, 0.0).astype(BF16)
        piece = dot(q, sel, 0, 0).astype(BF16)
        if d < 4:
            own_ref[d] = piece
        else:
            oth_ref[d - 4] = piece


def add_kernel(a_ref, b_ref, *outs):
    for d in range(4):
        outs[d][...] = a_ref[d] + b_ref[d]


def resident_kernel(len_ref, q_ref, c_ref, ks_ref, vs_ref, out_ref):
    base = pl.program_id(0) * 4
    lane = lax.broadcasted_iota(jnp.int32, (8, 256), 1)
    lane128 = lax.broadcasted_iota(jnp.int32, (8, 128), 1)
    for n in range(4):
        codes = c_ref[0, n, 0]
        ks = ks_ref[0, 0, n : n + 1, :] * (128.0**-0.5)
        vs = vs_ref[0, 0, n : n + 1, :]
        s = dot(q_ref[0, n], codes[:, :128], 1, 1) * ks
        live = lane < len_ref[base + n]
        s = jnp.where(live, s, -jnp.inf)
        m = jnp.max(s, axis=1, keepdims=True)
        e = jnp.exp(s - m)
        den = jnp.sum(e, axis=1, keepdims=True)
        acc = dot((e * vs).astype(BF16), codes[:, 128:], 1, 0)
        out_ref[pl.ds(n * 8, 8), :128] = acc
        out_ref[pl.ds(n * 8, 8), 128:] = jnp.where(lane128 == 0, m, den)


def resident(g, clen, queries, codes, ks, vs):
    return pl.pallas_call(
        resident_kernel,
        out_shape=jax.ShapeDtypeStruct((128, 256), F32),
        grid_spec=pltpu.PrefetchScalarGridSpec(
            num_scalar_prefetch=1,
            grid=(4,),
            in_specs=[
                pl.BlockSpec((1, 4, 8, 128), lambda i, s: (g, i, 0, 0)),
                pl.BlockSpec((1, 4, 1, 256, 256), lambda i, s: (g, i, 0, 0, 0)),
                pl.BlockSpec((1, 1, 4, 256), lambda i, s: (g, i, 0, 0)),
                pl.BlockSpec((1, 1, 4, 256), lambda i, s: (g, i, 0, 0)),
            ],
            out_specs=pl.BlockSpec((32, 256), lambda i, s: (i, 0)),
        ),
        compiler_params=pltpu.CompilerParams(vmem_limit_bytes=16 * 1024 * 1024),
        cost_estimate=pl.CostEstimate(flops=200_000_000, bytes_accessed=2_200_000, transcendentals=0),
    )(clen[g], queries, codes, ks, vs)


def group_max(v):
    lane = lax.broadcasted_iota(jnp.int32, v.shape, 1)
    n = v.shape[1]
    for s in (1, 2, 4, 8):
        other = jnp.where((lane & s) == 0, pltpu.roll(v, n - s, 1), pltpu.roll(v, s, 1))
        v = jnp.maximum(v, other)
    return v


def quantize(kv):
    largest = group_max(jnp.max(jnp.abs(kv), axis=0, keepdims=True))
    scale = (largest + 1e-6) / 127.0
    return (kv / scale).astype(BF16), scale


def block_kernel(core_ref, *refs):
    wa, wb, p, (q0, q1, q2, q3, out_ref) = refs[:4], refs[4:8], refs[8:17], refs[17:]
    feats = p[0].shape[0] // 4
    kv = None
    for k in range(4):
        rows = [p[s][pl.ds(k * feats, feats), :] for s in range(7)]
        rows.append(p[7 + k // 2][pl.ds((k % 2) * feats, feats), :])
        weight = jnp.concatenate([wa[k][...], wb[k][...]], axis=0)
        term = dot(weight, jnp.concatenate(rows, axis=0), 1, 0)
        kv = term if kv is None else kv + term
    first = core_ref[0] == 0
    key_codes, key_scale = quantize(jnp.where(first, kv[:128], kv[128:]))
    value_codes, value_scale = quantize(jnp.where(first, kv[128:], kv[:128]))
    q = q0[...] + q1[...] + q2[...] + q3[...]
    s = dot(q, key_codes, 0, 0) * (key_scale * (128.0**-0.5))
    row = lax.broadcasted_iota(jnp.int32, s.shape, 0)
    lane = lax.broadcasted_iota(jnp.int32, s.shape, 1)
    inside = (row >> 3) == (lane >> 4)
    s = jnp.where(inside, s, -jnp.inf)
    m = jnp.max(s, axis=1, keepdims=True)
    e = jnp.exp(s - m)
    den = jnp.sum(e, axis=1, keepdims=True)
    acc = dot((e * value_scale).astype(BF16), value_codes, 1, 1)
    stats = pack_columns(three(m) + three(den))
    out_ref[pl.ds(0, 128), :] = jnp.transpose(acc).astype(BF16)
    out_ref[pl.ds(128, 16), :] = jnp.transpose(stats)[:16].astype(BF16)


def pack_columns(columns):
    lane = lax.broadcasted_iota(jnp.int32, (columns[0].shape[0], 128), 1)
    out = jnp.zeros(lane.shape, F32)
    for i, c in enumerate(columns):
        out = jnp.where(lane == i, c, out)
    return out


def pack_rows(rows, height):
    sub = lax.broadcasted_iota(jnp.int32, (height, rows[0].shape[1]), 0)
    out = jnp.zeros(sub.shape, F32)
    for i, c in enumerate(rows):
        out = jnp.where(sub == i, c, out)
    return out


def join_kernel(code_ref, *refs):
    parts, out_ref = refs[:8], refs[8]
    stats = jnp.concatenate([r[pl.ds(128, 16), :].astype(F32) for r in parts], axis=0)
    columns = jnp.transpose(stats)
    codes = jnp.transpose(jnp.concatenate([code_ref[...].astype(F32), jnp.zeros((120, 128), F32)], axis=0))
    lane = lax.broadcasted_iota(jnp.int32, (128, 384), 1).astype(F32)
    top = jnp.full((1, 384), LOW, F32)
    joined, tops = [], []
    for b in range(8):
        c = [columns[:, b * 16 + i : b * 16 + i + 1] for i in range(6)]
        m = (c[0] + c[1]) + c[2]
        hit = codes[:, b : b + 1] == lane
        top = jnp.maximum(top, jnp.max(jnp.where(hit, m, LOW), axis=0, keepdims=True))
        joined.append(hit)
        tops.append((m, (c[3] + c[4]) + c[5]))
    den = jnp.zeros((1, 384), F32)
    acc = jnp.zeros((128, 384), F32)
    for b in range(8):
        m, d = tops[b]
        share = jnp.exp(jnp.where(joined[b], m - top, -jnp.inf))
        den = den + jnp.sum(share * d, axis=0, keepdims=True)
        acc = acc + dot(parts[b][pl.ds(0, 128), :], share.astype(BF16), 1, 0)
    out_ref[pl.ds(0, 128), :] = acc.astype(BF16)
    out_ref[pl.ds(128, 16), :] = pack_rows(three(top) + three(den), 16).astype(BF16)


def final_kernel(u0, u1, u2, u3, r0, r1, r2, out_ref, tmp):
    us = (u0, u1, u2, u3)
    tops, dens = [], []
    for u in us:
        rows = [u[pl.ds(128, 16), :].astype(F32)[i : i + 1] for i in range(6)]
        tops.append((rows[0] + rows[1]) + rows[2])
        dens.append((rows[3] + rows[4]) + rows[5])
    top = jnp.maximum(jnp.maximum(tops[0], tops[1]), jnp.maximum(tops[2], tops[3]))
    acc = jnp.zeros((128, 384), F32)
    den = jnp.zeros((1, 384), F32)
    for u, m, d in zip(us, tops, dens):
        share = jnp.exp(m - top)
        acc = acc + u[pl.ds(0, 128), :].astype(F32) * share
        den = den + d * share
    acc = jnp.transpose(acc)
    columns = jnp.transpose(pack_rows((top, den), 128))
    for g, r in enumerate((r0, r1, r2)):
        rows = slice(g * 128, g * 128 + 128)
        new_top, new_den = columns[rows, 0:1], columns[rows, 1:2]
        old_top, old_den = r[:, 128:129], r[:, 129:130]
        best = jnp.maximum(new_top, old_top)
        new_share, old_share = jnp.exp(new_top - best), jnp.exp(old_top - best)
        total = new_den * new_share + old_den * old_share
        tmp[pl.ds(g * 128, 128), :] = (acc[rows] * new_share + r[:, :128] * old_share) / total
    for q in range(8):
        out_ref[:, q * 128 : q * 128 + 128] = tmp[pl.ds(q, 48, stride=8), :].astype(BF16)


def shape(*dims, dtype=BF16):
    return jax.ShapeDtypeStruct(dims, dtype)


def role_shift(v, d):
    return lax.ppermute(v, "role", [(i, (i + d) % 4) for i in range(4)])


def x_shift(v, d):
    return lax.ppermute(v, "tensor", [(z * 4 + x, z * 4 + (x + d) % 4) for z in range(2) for x in range(4)])


def z_swap(v):
    return lax.ppermute(v, "tensor", [(t, (t + 4) % 8) for t in range(8)])


def zh_shift(v, d):
    return lax.ppermute(v, "batch", [(i, (i + 2 * d) % 8) for i in range(8)])


def core_swap(v):
    return lax.ppermute(v, "batch", [(i, i ^ 1) for i in range(8)])


def body(span, weight, queries, codes, scales, clen, bdest, brow):
    role = lax.axis_index("role")
    batch = lax.axis_index("batch")
    tensor = lax.axis_index("tensor")
    zh, core = batch // 2, batch % 2
    zl, x = tensor // 4, tensor % 4
    role1, core1 = role.reshape(1), core.reshape(1)
    tokens, feats = span.shape[0] // 4, span.shape[1]

    cut = call(cut_kernel, [shape(feats, tokens)] * 4, (role1, span), [SMEM, VMEM])
    own = jnp.concatenate([cut[0]] + [role_shift(cut[d], d) for d in (1, 2, 3)], axis=0)

    near = [(0, 0), (-1, 0), (1, 0), (0, 1), (2, 0), (1, 1), (-1, 1), (2, 1)]
    slots = jnp.stack([((zl + b) % 2) * 4 + (x + a) % 4 for a, b in near])
    half = [shape(128, weight.shape[0])] * 2
    wa0, wb0 = call(
        weight_kernel, half, (slots, core1, weight.reshape(weight.shape[0], 256)), [SMEM, SMEM, VMEM],
        scratch=[pltpu.VMEM((weight.shape[0], 256), F32)],
    )
    wa = [wa0] + [role_shift(wa0, d) for d in (1, 2, 3)]
    wb = [wb0] + [core_swap(v) for v in wa[1:]]

    dest = lax.dynamic_index_in_dim(bdest[:, 0].reshape(8, 4, 16), role, 1, keepdims=False)
    row = lax.dynamic_index_in_dim(brow.reshape(8, 4, 16), role, 1, keepdims=False)
    request = jnp.where(dest % 8 == batch, (dest // 8) * 16 + row, -1)
    lanes = jnp.repeat(request, 8, axis=1)
    lanes = jnp.where(lanes < 0, -1, lanes * 8 + jnp.arange(128, dtype=jnp.int32)[None, :] % 8)
    mine = jnp.stack([((zh + d) % 4) * 2 + core for d in range(4)])
    theirs = mine + 1 - 2 * core
    out_codes = lanes[jnp.concatenate([mine, theirs])]
    flat = queries.reshape(384, 128)
    q_own, q_oth = call(pick_kernel, [shape(4, 128, 128)] * 2, (out_codes, flat), [VMEM, VMEM])
    q_sum = call(add_kernel, [shape(128, 128)] * 4, (q_own, core_swap(q_oth)), [VMEM, VMEM])
    q_in = [q_sum[0]] + [zh_shift(q_sum[d], d) for d in (1, 2, 3)]

    ks = jnp.repeat(scales[:, :, 0, :, 0], BLOCK, axis=2).reshape(3, 4, 4, 256)
    vs = jnp.repeat(scales[:, :, 0, :, 1], BLOCK, axis=2).reshape(3, 4, 4, 256)
    res = [resident(g, clen, queries, codes, ks, vs) for g in range(3)]

    p1, p2, p3 = x_shift(own, 1), x_shift(own, -1), z_swap(own)
    p4, p5, p6 = x_shift(p1, 1), x_shift(p3, -1), z_swap(p1)
    cutoff = p6.shape[0] // 2
    p7a, p7b = x_shift(p6[:cutoff], 1), x_shift(p5[cutoff:], -1)

    blocks = call(
        block_kernel, shape(144, 128), (core1, *wa, *wb, own, p1, p2, p3, p4, p5, p6, p7a, p7b, *q_in),
        [SMEM] + [VMEM] * 21,
    )

    parts = [blocks] + [zh_shift(blocks, d) for d in (1, 2, 3)]
    parts = parts + [core_swap(v) for v in parts]
    origin = jnp.stack([((zh - d) % 4) * 2 + core for d in range(4)])
    in_codes = lanes[jnp.concatenate([origin, origin + 1 - 2 * core])]
    sums = call(join_kernel, shape(144, 384), (in_codes, *parts), [VMEM] * 9)
    sums = [sums] + [role_shift(sums, d) for d in (1, 2, 3)]
    out = call(
        final_kernel, shape(48, 1024), (*sums, *res), [VMEM] * 7, scratch=[pltpu.VMEM((384, 128), F32)]
    )
    return out.reshape(3, 16, 1024)


def solution(mesh):
    return jax.shard_map(
        body,
        mesh=mesh,
        in_specs=(
            P("batch", ("role", "tensor")),
            P("role", "tensor", None),
            P(None, "batch", "tensor", None),
            P(None, "batch", "tensor", None, None),
            P(None, "batch", "tensor", None, None),
            P(None, "batch"),
            P(),
            P(),
        ),
        out_specs=P(None, "batch", "tensor"),
        check_vma=False,
    )
```

```python
import jax
import jax.numpy as jnp
from jax import lax
from jax.experimental import pallas as pl
from jax.experimental.pallas import tpu as pltpu
from jax.sharding import PartitionSpec as P

BLOCK = 16
LOW = -1e38
STEPS = (0, 3, 1, 2)
F32 = jnp.float32
BF16 = jnp.bfloat16
VMEM = pl.BlockSpec(memory_space=pltpu.VMEM)
FETCH = pl.BlockSpec()
SMEM = pl.BlockSpec(memory_space=pltpu.SMEM)
ANY = pl.BlockSpec(memory_space=pl.ANY)
def call(kernel, outs, args, specs, scratch=(), cost=1.0):
    return pl.pallas_call(
        kernel,
        out_shape=outs,
        in_specs=specs,
        out_specs=jax.tree.map(lambda _: VMEM, outs),
        scratch_shapes=list(scratch),
        compiler_params=pltpu.CompilerParams(vmem_limit_bytes=48 * 1024 * 1024),
        cost_estimate=pl.CostEstimate(flops=0, bytes_accessed=int(cost * 3_000_000), transcendentals=0),
    )(*args)


def dot(a, b, ca, cb):
    return lax.dot_general(a, b, (((ca,), (cb,)), ((), ())), preferred_element_type=F32)


def three(v):
    hi = v.astype(BF16).astype(F32)
    mid = (v - hi).astype(BF16).astype(F32)
    return hi, mid, v - hi - mid


def pack_columns(columns):
    lane = lax.broadcasted_iota(jnp.int32, (columns[0].shape[0], 128), 1)
    out = jnp.zeros(lane.shape, F32)
    for i, c in enumerate(columns):
        out = jnp.where(lane == i, c, out)
    return out


def pack_rows(rows, height):
    sub = lax.broadcasted_iota(jnp.int32, (height, rows[0].shape[1]), 0)
    out = jnp.zeros(sub.shape, F32)
    for i, c in enumerate(rows):
        out = jnp.where(sub == i, c, out)
    return out


def weight_kernel(w_ref, x_ref, keep_ref, give_ref, p_ref, tmp):
    p_ref[...] = x_ref[...]
    tensor = lax.axis_index("tensor")
    zl, x = tensor // 4, lax.rem(tensor, 4)
    rows = w_ref.shape[0] // 8
    for b, out_ref in enumerate((keep_ref, give_ref)):
        for s in range(4):
            start = (lax.rem(zl + b, 2) * 4 + lax.rem(x + STEPS[s], 4)) * rows
            tmp[pl.ds(s * rows, rows), :] = w_ref[pl.ds(pl.multiple_of(start, rows), rows), :].astype(F32)
        out_ref[pl.ds(0, 128), :] = jnp.transpose(tmp[:, :128]).astype(BF16)
        out_ref[pl.ds(128, 128), :] = jnp.transpose(tmp[:, 128:]).astype(BF16)


def target_kernel(dest_ref, row_ref, out_ref):
    batch, role = lax.axis_index("batch"), lax.axis_index("role")
    lane = lax.broadcasted_iota(jnp.int32, (8, 512), 1)
    sub = lax.broadcasted_iota(jnp.int32, (8, 512), 0)
    block = lax.broadcasted_iota(jnp.int32, (512, 256), 0)
    place = lax.broadcasted_iota(jnp.int32, (512, 256), 1) >> 4
    pick = jnp.where((((block >> 4) & 3) == role) & ((block & 15) == place), 1.0, 0.0).astype(BF16)
    dest, row = [
        dot(jnp.where((lane >> 6) == sub, r[...], 0).astype(F32).astype(BF16), pick, 1, 0).astype(jnp.int32)
        for r in (dest_ref, row_ref)
    ]
    out_ref[...] = jnp.where((dest & 7) == batch, (dest >> 3) * 16 + row, -1)


def resident_kernel(len_ref, q_ref, sc_ref, c_ref, out_ref, buf, sems):
    copies = [
        pltpu.make_async_copy(c_ref.at[i // 2, pl.ds(i % 2 * 8, 8), 0], buf.at[i // 2, pl.ds(i % 2 * 8, 8)], sems.at[i])
        for i in range(6)
    ]
    for c in copies:
        c.start()
    lane = lax.broadcasted_iota(jnp.int32, (8, 256), 1)
    lane128 = lax.broadcasted_iota(jnp.int32, (128, 128), 1)
    column = lax.broadcasted_iota(jnp.int32, (16, 256), 0)
    block = lax.broadcasted_iota(jnp.int32, (16, 256), 1) >> 4
    pick = jnp.where(column == block, 1.0, 0.0).astype(BF16)
    for group in range(3):
        spread = []
        for half in range(2):
            parts = [p.astype(BF16) for p in three(sc_ref[pl.ds(group * 16, 16), half, :])]
            spread.append((dot(parts[0], pick, 1, 0) + dot(parts[1], pick, 1, 0)) + dot(parts[2], pick, 1, 0))
        ks, vs = spread[0] * (128.0**-0.5), spread[1]
        turned = jnp.transpose(jnp.concatenate([q_ref[group, n].astype(F32) for n in range(16)], axis=0))
        s = jnp.zeros((256, 128), F32)
        for n in range(0, 16, 2):
            if n % 8 == 0:
                copies[group * 2 + n // 8].wait()
            keys = jnp.concatenate([buf[group, n, :, :128], buf[group, n + 1, :, :128]], axis=1)
            own = [jnp.where((lane128 >> 3) == n + i, turned, 0.0).astype(BF16) for i in range(2)]
            s = s + dot(keys, jnp.concatenate(own, axis=0), 1, 0)
        s = jnp.transpose(s)
        scores, scale = [], []
        for n in range(16):
            live = lane < len_ref[group, n]
            scores.append(jnp.where(live, s[n * 8 : n * 8 + 8] * ks[n : n + 1], -jnp.inf))
            scale.append(jnp.broadcast_to(vs[n : n + 1], (8, 256)))
        s = jnp.concatenate(scores, axis=0)
        m = jnp.max(s, axis=1, keepdims=True)
        e = jnp.exp(s - m)
        den = jnp.sum(e, axis=1, keepdims=True)
        w = e * jnp.concatenate(scale, axis=0)
        for n in range(16):
            part = w[n * 8 : n * 8 + 8].astype(BF16)
            out_ref[pl.ds(group * 128 + n * 8, 8), :128] = dot(part, buf[group, n, :, 128:], 1, 0)
        out_ref[pl.ds(group * 128, 128), 128:] = jnp.where(lane128 == 0, m, den)


def project_kernel(w_ref, *refs):
    p, outs = refs[:5], refs[5:]
    role = lax.axis_index("role")
    count = p[0].shape[1] // 4
    for d in (2, 1, 3, 0):
        start = pl.multiple_of(lax.rem(role + d, 4) * count, 128)
        rows = jnp.concatenate([r[:, pl.ds(start, count)] for r in p], axis=0)
        outs[d][...] = dot(w_ref[...], rows, 1, 0).astype(outs[d].dtype)


def total_of(parts):
    a, b, c, d = [p[...].astype(F32) for p in parts]
    return (a + b) + (c + d)


def sum_kernel(a, b, c, d, out_ref):
    out_ref[...] = total_of((a, b, c, d)).astype(BF16)


def group_max(v):
    lane = lax.broadcasted_iota(jnp.int32, v.shape, 1)
    n = v.shape[1]
    for s in (1, 2, 4, 8):
        other = jnp.where((lane & s) == 0, pltpu.roll(v, n - s, 1), pltpu.roll(v, s, 1))
        v = jnp.maximum(v, other)
    return v


def quantize(kv):
    largest = group_max(jnp.max(jnp.abs(kv), axis=0, keepdims=True))
    scale = (largest + 1e-6) / 127.0
    return (kv / scale).astype(BF16), scale


def quantize_kernel(a, b, c, d, got, out_ref):
    kv = total_of((a, b, c, d)) + got[...].astype(F32)
    key_codes, key_scale = quantize(kv[:128])
    value_codes, value_scale = quantize(kv[128:])
    out_ref[pl.ds(0, 128), :] = key_codes
    out_ref[pl.ds(128, 128), :] = value_codes
    out_ref[pl.ds(256, 16), :] = pack_rows(three(key_scale) + three(value_scale), 16).astype(BF16)


def join_kernel(target_ref, q_ref, *refs):
    parts, out_ref, tmp = refs[:8], refs[8], refs[9]
    batch = lax.axis_index("batch")
    zh, core = batch // 2, lax.rem(batch, 2)
    q = q_ref[...]
    request = lax.broadcasted_iota(jnp.int32, (384, 256), 0) >> 3
    scales, top = [], jnp.full((384, 256), LOW, F32)
    for i in range(8):
        origin = lax.rem(zh + 4 - i % 4, 4) * 2 + (core if i < 4 else 1 - core)
        rows = parts[i][pl.ds(256, 16), :].astype(F32)
        key_scale = (rows[0:1] + rows[1:2]) + rows[2:3]
        scales.append((rows[3:4] + rows[4:5]) + rows[5:6])
        s = dot(q, parts[i][pl.ds(0, 128), :], 1, 0) * (key_scale * (128.0**-0.5))
        s = jnp.where(request == target_ref[pl.ds(origin, 1), :], s, -jnp.inf)
        tmp[i] = s
        top = jnp.maximum(top, s)
    top = jnp.max(top, axis=1, keepdims=True)
    total = jnp.zeros((384, 256), F32)
    acc = jnp.zeros((384, 128), F32)
    for i in range(8):
        e = jnp.exp(tmp[i] - top)
        total = total + e
        acc = acc + dot((e * scales[i]).astype(BF16), parts[i][pl.ds(128, 128), :], 1, 1)
    den = jnp.sum(total, axis=1, keepdims=True)
    out_ref[pl.ds(0, 128), :] = jnp.transpose(acc).astype(BF16)
    stats = pack_columns(three(top) + three(den))
    out_ref[pl.ds(128, 16), :] = jnp.transpose(stats)[:16].astype(BF16)


def final_kernel(u0, u1, u2, u3, r, out_ref, tmp):
    us = (u0, u1, u2, u3)
    tops, dens = [], []
    for u in us:
        rows = [u[pl.ds(128, 16), :].astype(F32)[i : i + 1] for i in range(6)]
        tops.append((rows[0] + rows[1]) + rows[2])
        dens.append((rows[3] + rows[4]) + rows[5])
    top = jnp.maximum(jnp.maximum(tops[0], tops[1]), jnp.maximum(tops[2], tops[3]))
    acc = jnp.zeros((128, 384), F32)
    den = jnp.zeros((1, 384), F32)
    for u, m, d in zip(us, tops, dens):
        share = jnp.exp(m - top)
        acc = acc + u[pl.ds(0, 128), :].astype(F32) * share
        den = den + d * share
    acc = jnp.transpose(acc)
    columns = jnp.transpose(pack_rows((top, den), 128))
    new_top, new_den = columns[:, 0:1], columns[:, 1:2]
    old_top, old_den = r[:, 128:129], r[:, 129:130]
    best = jnp.maximum(new_top, old_top)
    new_share, old_share = jnp.exp(new_top - best), jnp.exp(old_top - best)
    total = new_den * new_share + old_den * old_share
    tmp[...] = (acc * new_share + r[:, :128] * old_share) / total
    for q in range(8):
        out_ref[:, q * 128 : q * 128 + 128] = tmp[pl.ds(q, 48, stride=8), :].astype(BF16)


def shape(*dims, dtype=BF16):
    return jax.ShapeDtypeStruct(dims, dtype)


def role_shift(v, d):
    return lax.ppermute(v, "role", [(i, (i + d) % 4) for i in range(4)])


def x_shift(v, d):
    return lax.ppermute(v, "tensor", [(z * 4 + x, z * 4 + (x + d) % 4) for z in range(2) for x in range(4)])


def z_swap(v):
    return lax.ppermute(v, "tensor", [(t, (t + 4) % 8) for t in range(8)])


def zh_shift(v, d):
    return lax.ppermute(v, "batch", [(i, (i + 2 * d) % 8) for i in range(8)])


def core_swap(v):
    return lax.ppermute(v, "batch", [(i, i ^ 1) for i in range(8)])


def body(span, weight, queries, codes, scales, clen, bdest, brow):
    p0 = span.T
    p1, p2 = x_shift(p0, 1), x_shift(p0, -1)

    rows = weight.shape[0]
    keep, give, held = call(
        weight_kernel, [shape(256, rows // 2)] * 2 + [shape(*p0.shape)], (weight.reshape(rows, 256), p0), [FETCH] * 2,
        scratch=[pltpu.VMEM((rows // 2, 256), F32)],
    )
    got = z_swap(give)

    target = call(target_kernel, shape(8, 256, dtype=jnp.int32), (bdest.T, brow.reshape(1, 512)), [FETCH] * 2)
    (p1, p2), target = lax.optimization_barrier(((p1, p2), target))

    cutoff = p0.shape[0] // 2
    p3a, p3b = x_shift(p1[:cutoff], 1), x_shift(p2[cutoff:], -1)
    pieces = (held, p1, p2, p3a, p3b)

    count = p0.shape[1] // 4
    outs = [shape(256, count, dtype=F32 if d == 0 else BF16) for d in range(4)]
    far = call(project_kernel, outs, (got, *pieces), [VMEM] * 6)
    far_sums = [far[0]] + [role_shift(far[d], d) for d in (1, 2, 3)]
    pieces, _ = lax.optimization_barrier((pieces, far[0]))
    near = call(project_kernel, outs, (keep, *pieces), [VMEM] * 6)
    sums = [near[0]] + [role_shift(near[d], d) for d in (1, 2, 3)]
    back = z_swap(call(sum_kernel, shape(256, count), far_sums, [VMEM] * 4))
    codes_out = call(quantize_kernel, shape(272, count), (*sums, back), [VMEM] * 5)

    parts = [codes_out] + [zh_shift(codes_out, d) for d in (1, 2, 3)]
    parts = parts + [core_swap(v) for v in parts]
    sums = call(
        join_kernel, shape(144, 384), (target, queries.reshape(384, 128), *parts), [VMEM] * 10,
        scratch=[pltpu.VMEM((8, 384, 256), F32)], cost=2.5,
    )
    sums = [sums] + [role_shift(sums, d) for d in (1, 2, 3)]
    res = call(
        resident_kernel, shape(384, 256, dtype=F32), (clen, queries, jnp.swapaxes(scales, 3, 4).reshape(48, 2, 16), codes),
        [SMEM, VMEM, VMEM, ANY], scratch=[pltpu.VMEM((3, 16, 256, 256), BF16), pltpu.SemaphoreType.DMA((6,))], cost=5,
    )
    out = call(final_kernel, shape(48, 1024), (*sums, res), [VMEM] * 5, scratch=[pltpu.VMEM((384, 128), F32)])
    return out.reshape(3, 16, 1024)


def solution(mesh):
    return jax.shard_map(
        body,
        mesh=mesh,
        in_specs=(
            P("batch", ("role", "tensor")),
            P("role", "tensor", None),
            P(None, "batch", "tensor", None),
            P(None, "batch", "tensor", None, None),
            P(None, "batch", "tensor", None, None),
            P(None, "batch"),
            P(),
            P(),
        ),
        out_specs=P(None, "batch", "tensor"),
        check_vma=False,
    )
```

```python
import jax
import jax.numpy as jnp
from jax import lax
from jax.experimental import pallas as pl
from jax.experimental.pallas import tpu as pltpu
from jax.sharding import PartitionSpec as P

BLOCK = 16
LOW = -1e38
STEPS = (0, 3, 1, 2)
F32 = jnp.float32
BF16 = jnp.bfloat16
VMEM = pl.BlockSpec(memory_space=pltpu.VMEM)
FETCH = pl.BlockSpec()
SMEM = pl.BlockSpec(memory_space=pltpu.SMEM)
ANY = pl.BlockSpec(memory_space=pl.ANY)
def call(kernel, outs, args, specs, scratch=(), cost=1.0):
    return pl.pallas_call(
        kernel,
        out_shape=outs,
        in_specs=specs,
        out_specs=jax.tree.map(lambda _: VMEM, outs),
        scratch_shapes=list(scratch),
        compiler_params=pltpu.CompilerParams(vmem_limit_bytes=48 * 1024 * 1024),
        cost_estimate=pl.CostEstimate(flops=0, bytes_accessed=int(cost * 3_000_000), transcendentals=0),
    )(*args)


def dot(a, b, ca, cb):
    return lax.dot_general(a, b, (((ca,), (cb,)), ((), ())), preferred_element_type=F32)


def three(v):
    hi = v.astype(BF16).astype(F32)
    mid = (v - hi).astype(BF16).astype(F32)
    return hi, mid, v - hi - mid


def pack_columns(columns):
    lane = lax.broadcasted_iota(jnp.int32, (columns[0].shape[0], 128), 1)
    out = jnp.zeros(lane.shape, F32)
    for i, c in enumerate(columns):
        out = jnp.where(lane == i, c, out)
    return out


def pack_rows(rows, height):
    sub = lax.broadcasted_iota(jnp.int32, (height, rows[0].shape[1]), 0)
    out = jnp.zeros(sub.shape, F32)
    for i, c in enumerate(rows):
        out = jnp.where(sub == i, c, out)
    return out


def weight_kernel(w_ref, x_ref, keep_ref, give_ref, p_ref, tmp):
    p_ref[...] = x_ref[...]
    tensor = lax.axis_index("tensor")
    zl, x = tensor // 4, lax.rem(tensor, 4)
    rows = w_ref.shape[0] // 8
    for b, out_ref in enumerate((keep_ref, give_ref)):
        for s in range(4):
            start = (lax.rem(zl + b, 2) * 4 + lax.rem(x + STEPS[s], 4)) * rows
            tmp[pl.ds(s * rows, rows), :] = w_ref[pl.ds(pl.multiple_of(start, rows), rows), :].astype(F32)
        out_ref[pl.ds(0, 128), :] = jnp.transpose(tmp[:, :128]).astype(BF16)
        out_ref[pl.ds(128, 128), :] = jnp.transpose(tmp[:, 128:]).astype(BF16)


def target_kernel(dest_ref, row_ref, out_ref):
    batch, role = lax.axis_index("batch"), lax.axis_index("role")
    lane = lax.broadcasted_iota(jnp.int32, (8, 512), 1)
    sub = lax.broadcasted_iota(jnp.int32, (8, 512), 0)
    block = lax.broadcasted_iota(jnp.int32, (512, 256), 0)
    place = lax.broadcasted_iota(jnp.int32, (512, 256), 1) >> 4
    pick = jnp.where((((block >> 4) & 3) == role) & ((block & 15) == place), 1.0, 0.0).astype(BF16)
    dest, row = [
        dot(jnp.where((lane >> 6) == sub, r[...], 0).astype(F32).astype(BF16), pick, 1, 0).astype(jnp.int32)
        for r in (dest_ref, row_ref)
    ]
    out_ref[...] = jnp.where((dest & 7) == batch, (dest >> 3) * 16 + row, -1)


def resident_kernel(len_ref, q_ref, sc_ref, c_ref, out_ref, buf, sems):
    copies = [
        pltpu.make_async_copy(c_ref.at[i // 2, pl.ds(i % 2 * 8, 8), 0], buf.at[i // 2, pl.ds(i % 2 * 8, 8)], sems.at[i])
        for i in range(6)
    ]
    for c in copies:
        c.start()
    lane = lax.broadcasted_iota(jnp.int32, (8, 256), 1)
    lane128 = lax.broadcasted_iota(jnp.int32, (128, 128), 1)
    column = lax.broadcasted_iota(jnp.int32, (16, 256), 0)
    block = lax.broadcasted_iota(jnp.int32, (16, 256), 1) >> 4
    pick = jnp.where(column == block, 1.0, 0.0).astype(BF16)
    for group in range(3):
        spread = []
        for half in range(2):
            parts = [p.astype(BF16) for p in three(sc_ref[pl.ds(group * 16, 16), half, :])]
            spread.append((dot(parts[0], pick, 1, 0) + dot(parts[1], pick, 1, 0)) + dot(parts[2], pick, 1, 0))
        ks, vs = spread[0] * (128.0**-0.5), spread[1]
        turned = jnp.transpose(jnp.concatenate([q_ref[group, n].astype(F32) for n in range(16)], axis=0))
        s = jnp.zeros((256, 128), F32)
        for n in range(0, 16, 2):
            if n % 8 == 0:
                copies[group * 2 + n // 8].wait()
            keys = jnp.concatenate([buf[group, n, :, :128], buf[group, n + 1, :, :128]], axis=1)
            own = [jnp.where((lane128 >> 3) == n + i, turned, 0.0).astype(BF16) for i in range(2)]
            s = s + dot(keys, jnp.concatenate(own, axis=0), 1, 0)
        s = jnp.transpose(s)
        scores, scale = [], []
        for n in range(16):
            live = lane < len_ref[group, n]
            scores.append(jnp.where(live, s[n * 8 : n * 8 + 8] * ks[n : n + 1], -jnp.inf))
            scale.append(jnp.broadcast_to(vs[n : n + 1], (8, 256)))
        s = jnp.concatenate(scores, axis=0)
        m = jnp.max(s, axis=1, keepdims=True)
        e = jnp.exp(s - m)
        den = jnp.sum(e, axis=1, keepdims=True)
        w = e * jnp.concatenate(scale, axis=0)
        for n in range(16):
            part = w[n * 8 : n * 8 + 8].astype(BF16)
            out_ref[pl.ds(group * 128 + n * 8, 8), :128] = dot(part, buf[group, n, :, 128:], 1, 0)
        out_ref[pl.ds(group * 128, 128), 128:] = jnp.where(lane128 == 0, m, den)


def project_kernel(keep_ref, got_ref, *refs):
    p, out_ref = refs[:5], refs[5]
    zl = lax.axis_index("tensor") // 4
    count = p[0].shape[1] // 4
    for r in range(4):
        rows = jnp.concatenate([ref[:, pl.ds(r * count, count)] for ref in p], axis=0)
        out_ref[r * 2 + zl] = dot(keep_ref[...], rows, 1, 0).astype(BF16)
        out_ref[r * 2 + 1 - zl] = dot(got_ref[...], rows, 1, 0).astype(BF16)


def total_of(ref):
    a = [ref[i].astype(F32) for i in range(8)]
    return ((a[0] + a[1]) + (a[2] + a[3])) + ((a[4] + a[5]) + (a[6] + a[7]))


def group_max(v):
    lane = lax.broadcasted_iota(jnp.int32, v.shape, 1)
    n = v.shape[1]
    for s in (1, 2, 4, 8):
        other = jnp.where((lane & s) == 0, pltpu.roll(v, n - s, 1), pltpu.roll(v, s, 1))
        v = jnp.maximum(v, other)
    return v


def quantize(kv):
    largest = group_max(jnp.max(jnp.abs(kv), axis=0, keepdims=True))
    scale = (largest + 1e-6) / 127.0
    return (kv / scale).astype(BF16), scale


def quantize_kernel(sum_ref, out_ref):
    kv = total_of(sum_ref)
    key_codes, key_scale = quantize(kv[:128])
    value_codes, value_scale = quantize(kv[128:])
    out_ref[pl.ds(0, 128), :] = key_codes
    out_ref[pl.ds(128, 128), :] = value_codes
    out_ref[pl.ds(256, 16), :] = pack_rows(three(key_scale) + three(value_scale), 16).astype(BF16)


def join_kernel(target_ref, q_ref, *refs):
    parts, out_ref, tmp = refs[:8], refs[8], refs[9]
    batch = lax.axis_index("batch")
    zh, core = batch // 2, lax.rem(batch, 2)
    q = q_ref[...]
    request = lax.broadcasted_iota(jnp.int32, (384, 256), 0) >> 3
    scales, top = [], jnp.full((384, 256), LOW, F32)
    for i in range(8):
        origin = lax.rem(zh + 4 - i % 4, 4) * 2 + (core if i < 4 else 1 - core)
        rows = parts[i][pl.ds(256, 16), :].astype(F32)
        key_scale = (rows[0:1] + rows[1:2]) + rows[2:3]
        scales.append((rows[3:4] + rows[4:5]) + rows[5:6])
        s = dot(q, parts[i][pl.ds(0, 128), :], 1, 0) * (key_scale * (128.0**-0.5))
        s = jnp.where(request == target_ref[pl.ds(origin, 1), :], s, -jnp.inf)
        tmp[i] = s
        top = jnp.maximum(top, s)
    top = jnp.max(top, axis=1, keepdims=True)
    total = jnp.zeros((384, 256), F32)
    acc = jnp.zeros((384, 128), F32)
    for i in range(8):
        e = jnp.exp(tmp[i] - top)
        total = total + e
        acc = acc + dot((e * scales[i]).astype(BF16), parts[i][pl.ds(128, 128), :], 1, 1)
    den = jnp.sum(total, axis=1, keepdims=True)
    out_ref[pl.ds(0, 128), :] = jnp.transpose(acc).astype(BF16)
    stats = pack_columns(three(top) + three(den))
    out_ref[pl.ds(128, 16), :] = jnp.transpose(stats)[:16].astype(BF16)


def final_kernel(u0, u1, u2, u3, r, out_ref, tmp):
    us = (u0, u1, u2, u3)
    tops, dens = [], []
    for u in us:
        rows = [u[pl.ds(128, 16), :].astype(F32)[i : i + 1] for i in range(6)]
        tops.append((rows[0] + rows[1]) + rows[2])
        dens.append((rows[3] + rows[4]) + rows[5])
    top = jnp.maximum(jnp.maximum(tops[0], tops[1]), jnp.maximum(tops[2], tops[3]))
    acc = jnp.zeros((128, 384), F32)
    den = jnp.zeros((1, 384), F32)
    for u, m, d in zip(us, tops, dens):
        share = jnp.exp(m - top)
        acc = acc + u[pl.ds(0, 128), :].astype(F32) * share
        den = den + d * share
    acc = jnp.transpose(acc)
    columns = jnp.transpose(pack_rows((top, den), 128))
    new_top, new_den = columns[:, 0:1], columns[:, 1:2]
    old_top, old_den = r[:, 128:129], r[:, 129:130]
    best = jnp.maximum(new_top, old_top)
    new_share, old_share = jnp.exp(new_top - best), jnp.exp(old_top - best)
    total = new_den * new_share + old_den * old_share
    tmp[...] = (acc * new_share + r[:, :128] * old_share) / total
    for q in range(8):
        out_ref[:, q * 128 : q * 128 + 128] = tmp[pl.ds(q, 48, stride=8), :].astype(BF16)


def shape(*dims, dtype=BF16):
    return jax.ShapeDtypeStruct(dims, dtype)


def role_shift(v, d):
    return lax.ppermute(v, "role", [(i, (i + d) % 4) for i in range(4)])


def x_shift(v, d):
    return lax.ppermute(v, "tensor", [(z * 4 + x, z * 4 + (x + d) % 4) for z in range(2) for x in range(4)])


def z_swap(v):
    return lax.ppermute(v, "tensor", [(t, (t + 4) % 8) for t in range(8)])


def zh_shift(v, d):
    return lax.ppermute(v, "batch", [(i, (i + 2 * d) % 8) for i in range(8)])


def core_swap(v):
    return lax.ppermute(v, "batch", [(i, i ^ 1) for i in range(8)])


def body(span, weight, queries, codes, scales, clen, bdest, brow):
    p0 = span.T
    p1, p2 = x_shift(p0, 1), x_shift(p0, -1)

    rows = weight.shape[0]
    keep, give, held = call(
        weight_kernel, [shape(256, rows // 2)] * 2 + [shape(*p0.shape)], (weight.reshape(rows, 256), p0), [FETCH] * 2,
        scratch=[pltpu.VMEM((rows // 2, 256), F32)],
    )
    got = z_swap(give)

    target = call(target_kernel, shape(8, 256, dtype=jnp.int32), (bdest.T, brow.reshape(1, 512)), [FETCH] * 2)
    (p1, p2), target = lax.optimization_barrier(((p1, p2), target))

    cutoff = p0.shape[0] // 2
    p3a, p3b = x_shift(p1[:cutoff], 1), x_shift(p2[cutoff:], -1)
    pieces = (held, p1, p2, p3a, p3b)

    count = p0.shape[1] // 4
    outs = call(project_kernel, shape(8, 256, count), (keep, got, *pieces), [VMEM] * 7)
    groups = [[r * 8 + z * 4 + x for r in range(4) for z in range(2)] for x in range(4)]
    sums = lax.all_to_all(outs, ("role", "tensor"), 0, 0, axis_index_groups=groups)
    codes_out = call(quantize_kernel, shape(272, count), (sums,), [VMEM])

    parts = [codes_out] + [zh_shift(codes_out, d) for d in (1, 2, 3)]
    parts = parts + [core_swap(v) for v in parts]
    sums = call(
        join_kernel, shape(144, 384), (target, queries.reshape(384, 128), *parts), [VMEM] * 10,
        scratch=[pltpu.VMEM((8, 384, 256), F32)], cost=2.5,
    )
    sums = [sums] + [role_shift(sums, d) for d in (1, 2, 3)]
    res = call(
        resident_kernel, shape(384, 256, dtype=F32), (clen, queries, jnp.swapaxes(scales, 3, 4).reshape(48, 2, 16), codes),
        [SMEM, VMEM, VMEM, ANY], scratch=[pltpu.VMEM((3, 16, 256, 256), BF16), pltpu.SemaphoreType.DMA((6,))], cost=5,
    )
    out = call(final_kernel, shape(48, 1024), (*sums, res), [VMEM] * 5, scratch=[pltpu.VMEM((384, 128), F32)])
    return out.reshape(3, 16, 1024)


def solution(mesh):
    return jax.shard_map(
        body,
        mesh=mesh,
        in_specs=(
            P("batch", ("role", "tensor")),
            P("role", "tensor", None),
            P(None, "batch", "tensor", None),
            P(None, "batch", "tensor", None, None),
            P(None, "batch", "tensor", None, None),
            P(None, "batch"),
            P(),
            P(),
        ),
        out_specs=P(None, "batch", "tensor"),
        check_vma=False,
    )
```

```python
import jax
import jax.numpy as jnp
from jax import lax
from jax.experimental import pallas as pl
from jax.experimental.pallas import tpu as pltpu
from jax.sharding import PartitionSpec as P

BLOCK = 16
LOW = -1e38
STEPS = (0, 3, 1, 2)
F32 = jnp.float32
BF16 = jnp.bfloat16
VMEM = pl.BlockSpec(memory_space=pltpu.VMEM)
FETCH = pl.BlockSpec()
SMEM = pl.BlockSpec(memory_space=pltpu.SMEM)
ANY = pl.BlockSpec(memory_space=pl.ANY)
def call(kernel, outs, args, specs, scratch=(), cost=1.0):
    return pl.pallas_call(
        kernel,
        out_shape=outs,
        in_specs=specs,
        out_specs=jax.tree.map(lambda _: VMEM, outs),
        scratch_shapes=list(scratch),
        compiler_params=pltpu.CompilerParams(vmem_limit_bytes=48 * 1024 * 1024),
        cost_estimate=pl.CostEstimate(flops=0, bytes_accessed=int(cost * 3_000_000), transcendentals=0),
    )(*args)


def dot(a, b, ca, cb):
    return lax.dot_general(a, b, (((ca,), (cb,)), ((), ())), preferred_element_type=F32)


def three(v):
    hi = v.astype(BF16).astype(F32)
    mid = (v - hi).astype(BF16).astype(F32)
    return hi, mid, v - hi - mid


def pack_columns(columns):
    lane = lax.broadcasted_iota(jnp.int32, (columns[0].shape[0], 128), 1)
    out = jnp.zeros(lane.shape, F32)
    for i, c in enumerate(columns):
        out = jnp.where(lane == i, c, out)
    return out


def pack_rows(rows, height):
    sub = lax.broadcasted_iota(jnp.int32, (height, rows[0].shape[1]), 0)
    out = jnp.zeros(sub.shape, F32)
    for i, c in enumerate(rows):
        out = jnp.where(sub == i, c, out)
    return out


def weight_kernel(w_ref, x_ref, keep_ref, give_ref, p_ref, tmp):
    p_ref[...] = x_ref[...]
    tensor = lax.axis_index("tensor")
    zl, x = tensor // 4, lax.rem(tensor, 4)
    rows = w_ref.shape[0] // 8
    for b, out_ref in enumerate((keep_ref, give_ref)):
        for s in range(4):
            start = (lax.rem(zl + b, 2) * 4 + lax.rem(x + STEPS[s], 4)) * rows
            tmp[pl.ds(s * rows, rows), :] = w_ref[pl.ds(pl.multiple_of(start, rows), rows), :].astype(F32)
        out_ref[pl.ds(0, 128), :] = jnp.transpose(tmp[:, :128]).astype(BF16)
        out_ref[pl.ds(128, 128), :] = jnp.transpose(tmp[:, 128:]).astype(BF16)


def plan_kernel(dest_ref, row_ref, turn_ref, window_ref, target_ref, tmp):
    batch, role = lax.axis_index("batch"), lax.axis_index("role")
    zh = batch // 2
    dest = dest_ref[...]
    key = (dest & 7) >> 1
    index = lax.broadcasted_iota(jnp.int32, (1, 512), 1)
    key_i, order_i = key.astype(F32), (key * 512 + index).astype(F32)
    columns = jnp.transpose(pack_rows((key_i, order_i), 128))
    key_j, order_j = columns[:, 0:1], columns[:, 1:2]
    one = lax.broadcasted_iota(jnp.int32, (512, 512), 0)
    two = lax.broadcasted_iota(jnp.int32, (512, 512), 1)
    same = (one >> 6) == (two >> 6)
    rank = jnp.sum(jnp.where(same & (order_i < order_j), 1.0, 0.0), axis=1, keepdims=True).astype(jnp.int32)
    less = jnp.sum(jnp.where(same & (key_i < key_j), 1.0, 0.0), axis=1, keepdims=True).astype(jnp.int32)
    owner, slot = rank & 3, rank >> 2
    place = slot - ((less - owner + 3) >> 2)
    lane = lax.broadcasted_iota(jnp.int32, (512, 128), 1) >> 4
    pick = jnp.where((owner == role) & (place == lane), 1.0, 0.0).astype(BF16)
    request = jnp.where((dest & 7) == batch, (dest >> 3) * 16 + row_ref[...] + 1, 0)
    sub = lax.broadcasted_iota(jnp.int32, (8, 512), 0)
    spread = jnp.where((lax.broadcasted_iota(jnp.int32, (8, 512), 1) >> 6) == sub, request, 0)
    target_ref[...] = dot(spread.astype(F32).astype(BF16), pick, 1, 0).astype(jnp.int32) - 1
    gap = lax.broadcasted_iota(jnp.int32, (256, 128), 0) - lax.broadcasted_iota(jnp.int32, (256, 128), 1)
    for d in range(4):
        before = ((index >> 6) == batch) & (key < lax.rem(zh + d, 4))
        count = jnp.sum(jnp.where(before, 1.0, 0.0), axis=1, keepdims=True).astype(jnp.int32)
        window_ref[d] = jnp.where(gap == ((count - role + 3) >> 2) * 16, 1.0, 0.0).astype(BF16)
    tmp[...] = jnp.broadcast_to((owner * 16 + slot).astype(F32), (512, 128))
    own = tmp[pl.ds(pl.multiple_of(batch * 64, 64), 64), :].astype(BF16)
    token = lax.broadcasted_iota(jnp.int32, (1024, 64), 0)
    repeat = jnp.where((token >> 4) == lax.broadcasted_iota(jnp.int32, (1024, 64), 1), 1.0, 0.0).astype(BF16)
    to = dot(repeat, own, 1, 0).astype(jnp.int32)[:, 0:1] * 16 + (token[:, 0:1] & 15)
    turn_ref[...] = jnp.where(lax.broadcasted_iota(jnp.int32, (1024, 1024), 1) == to, 1.0, 0.0).astype(BF16)


def resident_kernel(len_ref, q_ref, sc_ref, c_ref, out_ref, buf, sems):
    copies = [
        pltpu.make_async_copy(c_ref.at[i // 2, pl.ds(i % 2 * 8, 8), 0], buf.at[i // 2, pl.ds(i % 2 * 8, 8)], sems.at[i])
        for i in range(6)
    ]
    for c in copies:
        c.start()
    lane = lax.broadcasted_iota(jnp.int32, (8, 256), 1)
    lane128 = lax.broadcasted_iota(jnp.int32, (128, 128), 1)
    column = lax.broadcasted_iota(jnp.int32, (16, 256), 0)
    block = lax.broadcasted_iota(jnp.int32, (16, 256), 1) >> 4
    pick = jnp.where(column == block, 1.0, 0.0).astype(BF16)
    for group in range(3):
        spread = []
        for half in range(2):
            parts = [p.astype(BF16) for p in three(sc_ref[pl.ds(group * 16, 16), half, :])]
            spread.append((dot(parts[0], pick, 1, 0) + dot(parts[1], pick, 1, 0)) + dot(parts[2], pick, 1, 0))
        ks, vs = spread[0] * (128.0**-0.5), spread[1]
        turned = jnp.transpose(jnp.concatenate([q_ref[group, n].astype(F32) for n in range(16)], axis=0))
        s = jnp.zeros((256, 128), F32)
        for n in range(0, 16, 2):
            if n % 8 == 0:
                copies[group * 2 + n // 8].wait()
            keys = jnp.concatenate([buf[group, n, :, :128], buf[group, n + 1, :, :128]], axis=1)
            own = [jnp.where((lane128 >> 3) == n + i, turned, 0.0).astype(BF16) for i in range(2)]
            s = s + dot(keys, jnp.concatenate(own, axis=0), 1, 0)
        s = jnp.transpose(s)
        scores, scale = [], []
        for n in range(16):
            live = lane < len_ref[group, n]
            scores.append(jnp.where(live, s[n * 8 : n * 8 + 8] * ks[n : n + 1], -jnp.inf))
            scale.append(jnp.broadcast_to(vs[n : n + 1], (8, 256)))
        s = jnp.concatenate(scores, axis=0)
        m = jnp.max(s, axis=1, keepdims=True)
        e = jnp.exp(s - m)
        den = jnp.sum(e, axis=1, keepdims=True)
        w = e * jnp.concatenate(scale, axis=0)
        for n in range(16):
            part = w[n * 8 : n * 8 + 8].astype(BF16)
            out_ref[pl.ds(group * 128 + n * 8, 8), :128] = dot(part, buf[group, n, :, 128:], 1, 0)
        out_ref[pl.ds(group * 128, 128), 128:] = jnp.where(lane128 == 0, m, den)


def project_kernel(keep_ref, got_ref, turn_ref, *refs):
    p, out_ref = refs[:5], refs[5]
    zl = lax.axis_index("tensor") // 4
    weight = jnp.concatenate([keep_ref[...], got_ref[...]], axis=0)
    kv = dot(weight, jnp.concatenate([ref[...] for ref in p], axis=0), 1, 0).astype(BF16)
    for r in range(4):
        part = dot(kv, turn_ref[:, r * 256 : r * 256 + 256], 1, 0).astype(BF16)
        out_ref[r * 2 + zl] = part[:256]
        out_ref[r * 2 + 1 - zl] = part[256:]


def total_of(ref):
    a = [ref[i].astype(F32) for i in range(8)]
    return ((a[0] + a[1]) + (a[2] + a[3])) + ((a[4] + a[5]) + (a[6] + a[7]))


def group_max(v):
    lane = lax.broadcasted_iota(jnp.int32, v.shape, 1)
    n = v.shape[1]
    for s in (1, 2, 4, 8):
        other = jnp.where((lane & s) == 0, pltpu.roll(v, n - s, 1), pltpu.roll(v, s, 1))
        v = jnp.maximum(v, other)
    return v


def quantize(kv):
    largest = group_max(jnp.max(jnp.abs(kv), axis=0, keepdims=True))
    scale = (largest + 1e-6) / 127.0
    return (kv / scale).astype(BF16), scale


def quantize_kernel(sum_ref, window_ref, *outs):
    kv = total_of(sum_ref)
    key_codes, key_scale = quantize(kv[:128])
    value_codes, value_scale = quantize(kv[128:])
    scales = pack_rows(three(key_scale) + three(value_scale), 16).astype(BF16)
    codes = jnp.concatenate([key_codes, value_codes, scales], axis=0)
    for d in range(4):
        outs[d][...] = dot(codes, window_ref[d], 1, 0).astype(BF16)


def join_kernel(target_ref, q_ref, *refs):
    parts, out_ref, tmp = refs[:8], refs[8], refs[9]
    batch = lax.axis_index("batch")
    zh, core = batch // 2, lax.rem(batch, 2)
    q = q_ref[...]
    request = lax.broadcasted_iota(jnp.int32, (384, 128), 0) >> 3
    scales, top = [], jnp.full((384, 128), LOW, F32)
    for i in range(8):
        origin = lax.rem(zh + 4 - i % 4, 4) * 2 + (core if i < 4 else 1 - core)
        rows = parts[i][pl.ds(256, 16), :].astype(F32)
        key_scale = (rows[0:1] + rows[1:2]) + rows[2:3]
        scales.append((rows[3:4] + rows[4:5]) + rows[5:6])
        s = dot(q, parts[i][pl.ds(0, 128), :], 1, 0) * (key_scale * (128.0**-0.5))
        s = jnp.where(request == target_ref[pl.ds(origin, 1), :], s, -jnp.inf)
        tmp[i] = s
        top = jnp.maximum(top, s)
    top = jnp.max(top, axis=1, keepdims=True)
    total = jnp.zeros((384, 128), F32)
    acc = jnp.zeros((384, 128), F32)
    for i in range(8):
        e = jnp.exp(tmp[i] - top)
        total = total + e
        acc = acc + dot((e * scales[i]).astype(BF16), parts[i][pl.ds(128, 128), :], 1, 1)
    den = jnp.sum(total, axis=1, keepdims=True)
    out_ref[pl.ds(0, 128), :] = jnp.transpose(acc).astype(BF16)
    stats = pack_columns(three(top) + three(den))
    out_ref[pl.ds(128, 16), :] = jnp.transpose(stats)[:16].astype(BF16)


def final_kernel(u0, u1, u2, u3, r, out_ref, tmp):
    us = (u0, u1, u2, u3)
    tops, dens = [], []
    for u in us:
        rows = [u[pl.ds(128, 16), :].astype(F32)[i : i + 1] for i in range(6)]
        tops.append((rows[0] + rows[1]) + rows[2])
        dens.append((rows[3] + rows[4]) + rows[5])
    top = jnp.maximum(jnp.maximum(tops[0], tops[1]), jnp.maximum(tops[2], tops[3]))
    acc = jnp.zeros((128, 384), F32)
    den = jnp.zeros((1, 384), F32)
    for u, m, d in zip(us, tops, dens):
        share = jnp.exp(m - top)
        acc = acc + u[pl.ds(0, 128), :].astype(F32) * share
        den = den + d * share
    acc = jnp.transpose(acc)
    columns = jnp.transpose(pack_rows((top, den), 128))
    new_top, new_den = columns[:, 0:1], columns[:, 1:2]
    old_top, old_den = r[:, 128:129], r[:, 129:130]
    best = jnp.maximum(new_top, old_top)
    new_share, old_share = jnp.exp(new_top - best), jnp.exp(old_top - best)
    total = new_den * new_share + old_den * old_share
    tmp[...] = (acc * new_share + r[:, :128] * old_share) / total
    for q in range(8):
        out_ref[:, q * 128 : q * 128 + 128] = tmp[pl.ds(q, 48, stride=8), :].astype(BF16)


def shape(*dims, dtype=BF16):
    return jax.ShapeDtypeStruct(dims, dtype)


def role_shift(v, d):
    return lax.ppermute(v, "role", [(i, (i + d) % 4) for i in range(4)])


def x_shift(v, d):
    return lax.ppermute(v, "tensor", [(z * 4 + x, z * 4 + (x + d) % 4) for z in range(2) for x in range(4)])


def z_swap(v):
    return lax.ppermute(v, "tensor", [(t, (t + 4) % 8) for t in range(8)])


def zh_shift(v, d):
    return lax.ppermute(v, "batch", [(i, (i + 2 * d) % 8) for i in range(8)])


def core_swap(v):
    return lax.ppermute(v, "batch", [(i, i ^ 1) for i in range(8)])


def body(span, weight, queries, codes, scales, clen, bdest, brow):
    p0 = span.T
    p1, p2 = x_shift(p0, 1), x_shift(p0, -1)

    rows = weight.shape[0]
    keep, give, held = call(
        weight_kernel, [shape(256, rows // 2)] * 2 + [shape(*p0.shape)], (weight.reshape(rows, 256), p0), [FETCH] * 2,
        scratch=[pltpu.VMEM((rows // 2, 256), F32)],
    )
    got = z_swap(give)

    turn, window, target = call(
        plan_kernel, [shape(1024, 1024), shape(4, 256, 128), shape(8, 128, dtype=jnp.int32)],
        (bdest.T, brow.reshape(1, 512)), [FETCH] * 2, scratch=[pltpu.VMEM((512, 128), F32)], cost=2,
    )
    (p1, p2), target = lax.optimization_barrier(((p1, p2), target))

    cutoff = p0.shape[0] // 2
    p3a, p3b = x_shift(p1[:cutoff], 1), x_shift(p2[cutoff:], -1)
    pieces = (held, p1, p2, p3a, p3b)

    count = p0.shape[1] // 4
    outs = call(project_kernel, shape(8, 256, count), (keep, got, turn, *pieces), [VMEM] * 8, cost=2)
    groups = [[r * 8 + z * 4 + x for r in range(4) for z in range(2)] for x in range(4)]
    sums = lax.all_to_all(outs, ("role", "tensor"), 0, 0, axis_index_groups=groups)
    cuts = call(quantize_kernel, [shape(272, 128)] * 4, (sums, window), [VMEM] * 2)

    parts = [cuts[0]] + [zh_shift(cuts[d], d) for d in (1, 2, 3)]
    parts = parts + [core_swap(v) for v in parts]
    sums = call(
        join_kernel, shape(144, 384), (target, queries.reshape(384, 128), *parts), [VMEM] * 10,
        scratch=[pltpu.VMEM((8, 384, 128), F32)], cost=1.5,
    )
    sums = [sums] + [role_shift(sums, d) for d in (1, 2, 3)]
    res = call(
        resident_kernel, shape(384, 256, dtype=F32), (clen, queries, jnp.swapaxes(scales, 3, 4).reshape(48, 2, 16), codes),
        [SMEM, VMEM, VMEM, ANY], scratch=[pltpu.VMEM((3, 16, 256, 256), BF16), pltpu.SemaphoreType.DMA((6,))], cost=5,
    )
    out = call(final_kernel, shape(48, 1024), (*sums, res), [VMEM] * 5, scratch=[pltpu.VMEM((384, 128), F32)])
    return out.reshape(3, 16, 1024)


def solution(mesh):
    return jax.shard_map(
        body,
        mesh=mesh,
        in_specs=(
            P("batch", ("role", "tensor")),
            P("role", "tensor", None),
            P(None, "batch", "tensor", None),
            P(None, "batch", "tensor", None, None),
            P(None, "batch", "tensor", None, None),
            P(None, "batch"),
            P(),
            P(),
        ),
        out_specs=P(None, "batch", "tensor"),
        check_vma=False,
    )
```

```python
import jax
import jax.numpy as jnp
from jax import lax
from jax.experimental import pallas as pl
from jax.experimental.pallas import tpu as pltpu
from jax.sharding import PartitionSpec as P

BLOCK = 16
LOW = -1e38
STEPS = (0, 3, 1, 2)
F32 = jnp.float32
BF16 = jnp.bfloat16
VMEM = pl.BlockSpec(memory_space=pltpu.VMEM)
FETCH = pl.BlockSpec()
SMEM = pl.BlockSpec(memory_space=pltpu.SMEM)
ANY = pl.BlockSpec(memory_space=pl.ANY)
def call(kernel, outs, args, specs, scratch=(), cost=1.0):
    return pl.pallas_call(
        kernel,
        out_shape=outs,
        in_specs=specs,
        out_specs=jax.tree.map(lambda _: VMEM, outs),
        scratch_shapes=list(scratch),
        compiler_params=pltpu.CompilerParams(vmem_limit_bytes=48 * 1024 * 1024),
        cost_estimate=pl.CostEstimate(flops=0, bytes_accessed=int(cost * 3_000_000), transcendentals=0),
    )(*args)


def dot(a, b, ca, cb):
    return lax.dot_general(a, b, (((ca,), (cb,)), ((), ())), preferred_element_type=F32)


def three(v):
    hi = v.astype(BF16).astype(F32)
    mid = (v - hi).astype(BF16).astype(F32)
    return hi, mid, v - hi - mid


def pack_columns(columns):
    lane = lax.broadcasted_iota(jnp.int32, (columns[0].shape[0], 128), 1)
    out = jnp.zeros(lane.shape, F32)
    for i, c in enumerate(columns):
        out = jnp.where(lane == i, c, out)
    return out


def pack_rows(rows, height):
    sub = lax.broadcasted_iota(jnp.int32, (height, rows[0].shape[1]), 0)
    out = jnp.zeros(sub.shape, F32)
    for i, c in enumerate(rows):
        out = jnp.where(sub == i, c, out)
    return out


def weight_kernel(w_ref, x_ref, keep_ref, give_ref, p_ref, tmp):
    p_ref[...] = x_ref[...]
    tensor = lax.axis_index("tensor")
    zl, x = tensor // 4, lax.rem(tensor, 4)
    rows = w_ref.shape[0] // 8
    for b, out_ref in enumerate((keep_ref, give_ref)):
        for s in range(4):
            start = (lax.rem(zl + b, 2) * 4 + lax.rem(x + STEPS[s], 4)) * rows
            tmp[pl.ds(s * rows, rows), :] = w_ref[pl.ds(pl.multiple_of(start, rows), rows), :].astype(F32)
        out_ref[pl.ds(0, 128), :] = jnp.transpose(tmp[:, :128]).astype(BF16)
        out_ref[pl.ds(128, 128), :] = jnp.transpose(tmp[:, 128:]).astype(BF16)


def plan_kernel(dest_ref, row_ref, turn_ref, window_ref, target_ref, tmp):
    batch, role = lax.axis_index("batch"), lax.axis_index("role")
    zh = batch // 2
    dest = dest_ref[...]
    key = (dest & 7) >> 1
    index = lax.broadcasted_iota(jnp.int32, (1, 512), 1)
    key_i, order_i = key.astype(F32), (key * 512 + index).astype(F32)
    columns = jnp.transpose(pack_rows((key_i, order_i), 128))
    key_j, order_j = columns[:, 0:1], columns[:, 1:2]
    one = lax.broadcasted_iota(jnp.int32, (512, 512), 0)
    two = lax.broadcasted_iota(jnp.int32, (512, 512), 1)
    same = (one >> 6) == (two >> 6)
    rank = jnp.sum(jnp.where(same & (order_i < order_j), 1.0, 0.0), axis=1, keepdims=True).astype(jnp.int32)
    less = jnp.sum(jnp.where(same & (key_i < key_j), 1.0, 0.0), axis=1, keepdims=True).astype(jnp.int32)
    owner, slot = rank & 3, rank >> 2
    place = slot - ((less - owner + 3) >> 2)
    lane = lax.broadcasted_iota(jnp.int32, (512, 128), 1) >> 4
    pick = jnp.where((owner == role) & (place == lane), 1.0, 0.0).astype(BF16)
    request = jnp.where((dest & 7) == batch, (dest >> 3) * 16 + row_ref[...] + 1, 0)
    sub = lax.broadcasted_iota(jnp.int32, (8, 512), 0)
    spread = jnp.where((lax.broadcasted_iota(jnp.int32, (8, 512), 1) >> 6) == sub, request, 0)
    target_ref[...] = dot(spread.astype(F32).astype(BF16), pick, 1, 0).astype(jnp.int32) - 1
    gap = lax.broadcasted_iota(jnp.int32, (256, 128), 0) - lax.broadcasted_iota(jnp.int32, (256, 128), 1)
    for d in range(4):
        before = ((index >> 6) == batch) & (key < lax.rem(zh + d, 4))
        count = jnp.sum(jnp.where(before, 1.0, 0.0), axis=1, keepdims=True).astype(jnp.int32)
        window_ref[d] = jnp.where(gap == ((count - role + 3) >> 2) * 16, 1.0, 0.0).astype(BF16)
    tmp[...] = jnp.broadcast_to((owner * 16 + slot).astype(F32), (512, 128))
    own = tmp[pl.ds(pl.multiple_of(batch * 64, 64), 64), :].astype(BF16)
    token = lax.broadcasted_iota(jnp.int32, (1024, 64), 0)
    repeat = jnp.where((token >> 4) == lax.broadcasted_iota(jnp.int32, (1024, 64), 1), 1.0, 0.0).astype(BF16)
    to = dot(repeat, own, 1, 0).astype(jnp.int32)[:, 0:1] * 16 + (token[:, 0:1] & 15)
    turn_ref[...] = jnp.where(lax.broadcasted_iota(jnp.int32, (1024, 1024), 1) == to, 1.0, 0.0).astype(BF16)


def resident_kernel(len_ref, q_ref, sc_ref, c_ref, out_ref, buf, sems):
    copies = [
        pltpu.make_async_copy(c_ref.at[i // 2, pl.ds(i % 2 * 8, 8), 0], buf.at[i // 2, pl.ds(i % 2 * 8, 8)], sems.at[i])
        for i in range(6)
    ]
    for c in copies:
        c.start()
    lane = lax.broadcasted_iota(jnp.int32, (8, 256), 1)
    lane128 = lax.broadcasted_iota(jnp.int32, (128, 128), 1)
    column = lax.broadcasted_iota(jnp.int32, (16, 256), 0)
    block = lax.broadcasted_iota(jnp.int32, (16, 256), 1) >> 4
    pick = jnp.where(column == block, 1.0, 0.0).astype(BF16)
    for group in range(3):
        spread = []
        for half in range(2):
            parts = [p.astype(BF16) for p in three(sc_ref[pl.ds(group * 16, 16), half, :])]
            spread.append((dot(parts[0], pick, 1, 0) + dot(parts[1], pick, 1, 0)) + dot(parts[2], pick, 1, 0))
        ks, vs = spread[0] * (128.0**-0.5), spread[1]
        turned = jnp.transpose(jnp.concatenate([q_ref[group, n].astype(F32) for n in range(16)], axis=0))
        s = jnp.zeros((256, 128), F32)
        for n in range(0, 16, 2):
            if n % 8 == 0:
                copies[group * 2 + n // 8].wait()
            keys = jnp.concatenate([buf[group, n, :, :128], buf[group, n + 1, :, :128]], axis=1)
            own = [jnp.where((lane128 >> 3) == n + i, turned, 0.0).astype(BF16) for i in range(2)]
            s = s + dot(keys, jnp.concatenate(own, axis=0), 1, 0)
        s = jnp.transpose(s)
        scores, scale = [], []
        for n in range(16):
            live = lane < len_ref[group, n]
            scores.append(jnp.where(live, s[n * 8 : n * 8 + 8] * ks[n : n + 1], -jnp.inf))
            scale.append(jnp.broadcast_to(vs[n : n + 1], (8, 256)))
        s = jnp.concatenate(scores, axis=0)
        m = jnp.max(s, axis=1, keepdims=True)
        e = jnp.exp(s - m)
        den = jnp.sum(e, axis=1, keepdims=True)
        w = e * jnp.concatenate(scale, axis=0)
        for n in range(16):
            part = w[n * 8 : n * 8 + 8].astype(BF16)
            out_ref[pl.ds(group * 128 + n * 8, 8), :128] = dot(part, buf[group, n, :, 128:], 1, 0)
        out_ref[pl.ds(group * 128, 128), 128:] = jnp.where(lane128 == 0, m, den)


def deal_kernel(turn_ref, p0, p1, p2, out_ref):
    rows = jnp.concatenate([p0[...], p1[...], p2[...]], axis=0)
    for r in range(4):
        out_ref[:, r * 256 : r * 256 + 256] = dot(rows, turn_ref[:, r * 256 : r * 256 + 256], 1, 0).astype(BF16)


def project_kernel(keep_ref, got_ref, turn_ref, early_ref, p3a, p3b, out_ref):
    zl = lax.axis_index("tensor") // 4
    weight = jnp.concatenate([keep_ref[...], got_ref[...]], axis=0)
    last = jnp.concatenate([p3a[...], p3b[...]], axis=0)
    for r in range(4):
        part = dot(last, turn_ref[:, r * 256 : r * 256 + 256], 1, 0).astype(BF16)
        rows = jnp.concatenate([early_ref[:, r * 256 : r * 256 + 256], part], axis=0)
        kv = dot(weight, rows, 1, 0).astype(BF16)
        out_ref[r * 2 + zl] = kv[:256]
        out_ref[r * 2 + 1 - zl] = kv[256:]


def total_of(ref):
    a = [ref[i].astype(F32) for i in range(8)]
    return ((a[0] + a[1]) + (a[2] + a[3])) + ((a[4] + a[5]) + (a[6] + a[7]))


def group_max(v):
    lane = lax.broadcasted_iota(jnp.int32, v.shape, 1)
    n = v.shape[1]
    for s in (1, 2, 4, 8):
        other = jnp.where((lane & s) == 0, pltpu.roll(v, n - s, 1), pltpu.roll(v, s, 1))
        v = jnp.maximum(v, other)
    return v


def quantize(kv):
    largest = group_max(jnp.max(jnp.abs(kv), axis=0, keepdims=True))
    scale = (largest + 1e-6) / 127.0
    return (kv / scale).astype(BF16), scale


def quantize_kernel(sum_ref, window_ref, *outs):
    kv = total_of(sum_ref)
    key_codes, key_scale = quantize(kv[:128])
    value_codes, value_scale = quantize(kv[128:])
    scales = pack_rows(three(key_scale) + three(value_scale), 16).astype(BF16)
    codes = jnp.concatenate([key_codes, value_codes, scales], axis=0)
    for d in range(4):
        outs[d][...] = dot(codes, window_ref[d], 1, 0).astype(BF16)


def join_kernel(target_ref, q_ref, *refs):
    parts, out_ref, tmp = refs[:8], refs[8], refs[9]
    batch = lax.axis_index("batch")
    zh, core = batch // 2, lax.rem(batch, 2)
    q = q_ref[...]
    request = lax.broadcasted_iota(jnp.int32, (384, 128), 0) >> 3
    scales, top = [], jnp.full((384, 128), LOW, F32)
    for i in range(8):
        origin = lax.rem(zh + 4 - i % 4, 4) * 2 + (core if i < 4 else 1 - core)
        rows = parts[i][pl.ds(256, 16), :].astype(F32)
        key_scale = (rows[0:1] + rows[1:2]) + rows[2:3]
        scales.append((rows[3:4] + rows[4:5]) + rows[5:6])
        s = dot(q, parts[i][pl.ds(0, 128), :], 1, 0) * (key_scale * (128.0**-0.5))
        s = jnp.where(request == target_ref[pl.ds(origin, 1), :], s, -jnp.inf)
        tmp[i] = s
        top = jnp.maximum(top, s)
    top = jnp.max(top, axis=1, keepdims=True)
    total = jnp.zeros((384, 128), F32)
    acc = jnp.zeros((384, 128), F32)
    for i in range(8):
        e = jnp.exp(tmp[i] - top)
        total = total + e
        acc = acc + dot((e * scales[i]).astype(BF16), parts[i][pl.ds(128, 128), :], 1, 1)
    den = jnp.sum(total, axis=1, keepdims=True)
    out_ref[pl.ds(0, 128), :] = jnp.transpose(acc).astype(BF16)
    stats = pack_columns(three(top) + three(den))
    out_ref[pl.ds(128, 16), :] = jnp.transpose(stats)[:16].astype(BF16)


def final_kernel(u0, u1, u2, u3, r, out_ref, tmp):
    us = (u0, u1, u2, u3)
    tops, dens = [], []
    for u in us:
        rows = [u[pl.ds(128, 16), :].astype(F32)[i : i + 1] for i in range(6)]
        tops.append((rows[0] + rows[1]) + rows[2])
        dens.append((rows[3] + rows[4]) + rows[5])
    top = jnp.maximum(jnp.maximum(tops[0], tops[1]), jnp.maximum(tops[2], tops[3]))
    acc = jnp.zeros((128, 384), F32)
    den = jnp.zeros((1, 384), F32)
    for u, m, d in zip(us, tops, dens):
        share = jnp.exp(m - top)
        acc = acc + u[pl.ds(0, 128), :].astype(F32) * share
        den = den + d * share
    acc = jnp.transpose(acc)
    columns = jnp.transpose(pack_rows((top, den), 128))
    new_top, new_den = columns[:, 0:1], columns[:, 1:2]
    old_top, old_den = r[:, 128:129], r[:, 129:130]
    best = jnp.maximum(new_top, old_top)
    new_share, old_share = jnp.exp(new_top - best), jnp.exp(old_top - best)
    total = new_den * new_share + old_den * old_share
    tmp[...] = (acc * new_share + r[:, :128] * old_share) / total
    for q in range(8):
        out_ref[:, q * 128 : q * 128 + 128] = tmp[pl.ds(q, 48, stride=8), :].astype(BF16)


def shape(*dims, dtype=BF16):
    return jax.ShapeDtypeStruct(dims, dtype)


def role_shift(v, d):
    return lax.ppermute(v, "role", [(i, (i + d) % 4) for i in range(4)])


def x_shift(v, d):
    return lax.ppermute(v, "tensor", [(z * 4 + x, z * 4 + (x + d) % 4) for z in range(2) for x in range(4)])


def z_swap(v):
    return lax.ppermute(v, "tensor", [(t, (t + 4) % 8) for t in range(8)])


def zh_shift(v, d):
    return lax.ppermute(v, "batch", [(i, (i + 2 * d) % 8) for i in range(8)])


def core_swap(v):
    return lax.ppermute(v, "batch", [(i, i ^ 1) for i in range(8)])


def body(span, weight, queries, codes, scales, clen, bdest, brow):
    p0 = span.T
    p1, p2 = x_shift(p0, 1), x_shift(p0, -1)

    rows = weight.shape[0]
    keep, give, held = call(
        weight_kernel, [shape(256, rows // 2)] * 2 + [shape(*p0.shape)], (weight.reshape(rows, 256), p0), [FETCH] * 2,
        scratch=[pltpu.VMEM((rows // 2, 256), F32)],
    )
    got = z_swap(give)

    turn, window, target = call(
        plan_kernel, [shape(1024, 1024), shape(4, 256, 128), shape(8, 128, dtype=jnp.int32)],
        (bdest.T, brow.reshape(1, 512)), [FETCH] * 2, scratch=[pltpu.VMEM((512, 128), F32)], cost=2,
    )
    (p1, p2), target = lax.optimization_barrier(((p1, p2), target))

    cutoff = p0.shape[0] // 2
    p3a, p3b = x_shift(p1[:cutoff], 1), x_shift(p2[cutoff:], -1)

    count = p0.shape[1] // 4
    early = call(deal_kernel, shape(3 * p0.shape[0], p0.shape[1]), (turn, held, p1, p2), [VMEM] * 4, cost=1.5)
    outs = call(project_kernel, shape(8, 256, count), (keep, got, turn, early, p3a, p3b), [VMEM] * 6)
    groups = [[r * 8 + z * 4 + x for r in range(4) for z in range(2)] for x in range(4)]
    sums = lax.all_to_all(outs, ("role", "tensor"), 0, 0, axis_index_groups=groups)
    cuts = call(quantize_kernel, [shape(272, 128)] * 4, (sums, window), [VMEM] * 2)

    parts = [cuts[0]] + [zh_shift(cuts[d], d) for d in (1, 2, 3)]
    parts = parts + [core_swap(v) for v in parts]
    sums = call(
        join_kernel, shape(144, 384), (target, queries.reshape(384, 128), *parts), [VMEM] * 10,
        scratch=[pltpu.VMEM((8, 384, 128), F32)], cost=1.5,
    )
    sums = [sums] + [role_shift(sums, d) for d in (1, 2, 3)]
    res = call(
        resident_kernel, shape(384, 256, dtype=F32), (clen, queries, jnp.swapaxes(scales, 3, 4).reshape(48, 2, 16), codes),
        [SMEM, VMEM, VMEM, ANY], scratch=[pltpu.VMEM((3, 16, 256, 256), BF16), pltpu.SemaphoreType.DMA((6,))], cost=5,
    )
    out = call(final_kernel, shape(48, 1024), (*sums, res), [VMEM] * 5, scratch=[pltpu.VMEM((384, 128), F32)])
    return out.reshape(3, 16, 1024)


def solution(mesh):
    return jax.shard_map(
        body,
        mesh=mesh,
        in_specs=(
            P("batch", ("role", "tensor")),
            P("role", "tensor", None),
            P(None, "batch", "tensor", None),
            P(None, "batch", "tensor", None, None),
            P(None, "batch", "tensor", None, None),
            P(None, "batch"),
            P(),
            P(),
        ),
        out_specs=P(None, "batch", "tensor"),
        check_vma=False,
    )
```

```python
import jax
import jax.numpy as jnp
from jax import lax
from jax.experimental import pallas as pl
from jax.experimental.pallas import tpu as pltpu
from jax.sharding import PartitionSpec as P

BLOCK = 16
LOW = -1e38
STEPS = (0, 3, 1, 2)
F32 = jnp.float32
BF16 = jnp.bfloat16
VMEM = pl.BlockSpec(memory_space=pltpu.VMEM)
FETCH = pl.BlockSpec()
SMEM = pl.BlockSpec(memory_space=pltpu.SMEM)
ANY = pl.BlockSpec(memory_space=pl.ANY)
def call(kernel, outs, args, specs, scratch=(), cost=1.0):
    return pl.pallas_call(
        kernel,
        out_shape=outs,
        in_specs=specs,
        out_specs=jax.tree.map(lambda _: VMEM, outs),
        scratch_shapes=list(scratch),
        compiler_params=pltpu.CompilerParams(vmem_limit_bytes=48 * 1024 * 1024),
        cost_estimate=pl.CostEstimate(flops=0, bytes_accessed=int(cost * 3_000_000), transcendentals=0),
    )(*args)


def dot(a, b, ca, cb):
    return lax.dot_general(a, b, (((ca,), (cb,)), ((), ())), preferred_element_type=F32)


def three(v):
    hi = v.astype(BF16).astype(F32)
    mid = (v - hi).astype(BF16).astype(F32)
    return hi, mid, v - hi - mid


def pack_columns(columns):
    lane = lax.broadcasted_iota(jnp.int32, (columns[0].shape[0], 128), 1)
    out = jnp.zeros(lane.shape, F32)
    for i, c in enumerate(columns):
        out = jnp.where(lane == i, c, out)
    return out


def pack_rows(rows, height):
    sub = lax.broadcasted_iota(jnp.int32, (height, rows[0].shape[1]), 0)
    out = jnp.zeros(sub.shape, F32)
    for i, c in enumerate(rows):
        out = jnp.where(sub == i, c, out)
    return out


def weight_kernel(w_ref, x_ref, keep_ref, give_ref, p_ref, tmp):
    p_ref[...] = x_ref[...]
    tensor = lax.axis_index("tensor")
    zl, x = tensor // 4, lax.rem(tensor, 4)
    rows = w_ref.shape[0] // 8
    for b, out_ref in enumerate((keep_ref, give_ref)):
        for s in range(4):
            start = (lax.rem(zl + b, 2) * 4 + lax.rem(x + STEPS[s], 4)) * rows
            tmp[pl.ds(s * rows, rows), :] = w_ref[pl.ds(pl.multiple_of(start, rows), rows), :].astype(F32)
        out_ref[pl.ds(0, 128), :] = jnp.transpose(tmp[:, :128]).astype(BF16)
        out_ref[pl.ds(128, 128), :] = jnp.transpose(tmp[:, 128:]).astype(BF16)


def plan_kernel(dest_ref, row_ref, turn_ref, window_ref, target_ref, tmp):
    batch, role = lax.axis_index("batch"), lax.axis_index("role")
    zh = batch // 2
    dest = dest_ref[...]
    key = (dest & 7) >> 1
    index = lax.broadcasted_iota(jnp.int32, (1, 512), 1)
    key_i, order_i = key.astype(F32), (key * 512 + index).astype(F32)
    columns = jnp.transpose(pack_rows((key_i, order_i), 128))
    key_j, order_j = columns[:, 0:1], columns[:, 1:2]
    one = lax.broadcasted_iota(jnp.int32, (512, 512), 0)
    two = lax.broadcasted_iota(jnp.int32, (512, 512), 1)
    same = (one >> 6) == (two >> 6)
    rank = jnp.sum(jnp.where(same & (order_i < order_j), 1.0, 0.0), axis=1, keepdims=True).astype(jnp.int32)
    less = jnp.sum(jnp.where(same & (key_i < key_j), 1.0, 0.0), axis=1, keepdims=True).astype(jnp.int32)
    owner, slot = rank & 3, rank >> 2
    place = slot - ((less - owner + 3) >> 2)
    lane = lax.broadcasted_iota(jnp.int32, (512, 128), 1) >> 4
    pick = jnp.where((owner == role) & (place == lane), 1.0, 0.0).astype(BF16)
    request = jnp.where((dest & 7) == batch, (dest >> 3) * 16 + row_ref[...] + 1, 0)
    sub = lax.broadcasted_iota(jnp.int32, (8, 512), 0)
    spread = jnp.where((lax.broadcasted_iota(jnp.int32, (8, 512), 1) >> 6) == sub, request, 0)
    target_ref[...] = dot(spread.astype(F32).astype(BF16), pick, 1, 0).astype(jnp.int32) - 1
    gap = lax.broadcasted_iota(jnp.int32, (256, 128), 0) - lax.broadcasted_iota(jnp.int32, (256, 128), 1)
    for d in range(4):
        before = ((index >> 6) == batch) & (key < lax.rem(zh + d, 4))
        count = jnp.sum(jnp.where(before, 1.0, 0.0), axis=1, keepdims=True).astype(jnp.int32)
        window_ref[d] = jnp.where(gap == ((count - role + 3) >> 2) * 16, 1.0, 0.0).astype(BF16)
    tmp[...] = jnp.broadcast_to((owner * 16 + slot).astype(F32), (512, 128))
    own = tmp[pl.ds(pl.multiple_of(batch * 64, 64), 64), :].astype(BF16)
    token = lax.broadcasted_iota(jnp.int32, (1024, 64), 0)
    repeat = jnp.where((token >> 4) == lax.broadcasted_iota(jnp.int32, (1024, 64), 1), 1.0, 0.0).astype(BF16)
    to = dot(repeat, own, 1, 0).astype(jnp.int32)[:, 0:1] * 16 + (token[:, 0:1] & 15)
    turn_ref[...] = jnp.where(lax.broadcasted_iota(jnp.int32, (1024, 1024), 1) == to, 1.0, 0.0).astype(BF16)


def resident_kernel(len_ref, q_ref, sc_ref, c_ref, out_ref, buf, sems):
    copies = [
        pltpu.make_async_copy(c_ref.at[i, :, 0], buf.at[i], sems.at[i])
        for i in range(3)
    ]
    for c in copies:
        c.start()
    lane = lax.broadcasted_iota(jnp.int32, (8, 256), 1)
    lane128 = lax.broadcasted_iota(jnp.int32, (128, 128), 1)
    column = lax.broadcasted_iota(jnp.int32, (16, 256), 0)
    block = lax.broadcasted_iota(jnp.int32, (16, 256), 1) >> 4
    pick = jnp.where(column == block, 1.0, 0.0).astype(BF16)
    for group in range(3):
        spread = []
        for half in range(2):
            parts = [p.astype(BF16) for p in three(sc_ref[pl.ds(group * 16, 16), half, :])]
            spread.append((dot(parts[0], pick, 1, 0) + dot(parts[1], pick, 1, 0)) + dot(parts[2], pick, 1, 0))
        ks, vs = spread[0] * (128.0**-0.5), spread[1]
        turned = jnp.transpose(q_ref[pl.ds(group * 128, 128), :].astype(F32))
        copies[group].wait()
        s = jnp.zeros((256, 128), F32)
        for n in range(0, 16, 2):
            keys = jnp.concatenate([buf[group, n, :, :128], buf[group, n + 1, :, :128]], axis=1)
            own = [jnp.where((lane128 >> 3) == n + i, turned, 0.0).astype(BF16) for i in range(2)]
            s = s + dot(keys, jnp.concatenate(own, axis=0), 1, 0)
        s = jnp.transpose(s)
        scores, scale = [], []
        for n in range(16):
            live = lane < len_ref[group, n]
            scores.append(jnp.where(live, s[n * 8 : n * 8 + 8] * ks[n : n + 1], -jnp.inf))
            scale.append(jnp.broadcast_to(vs[n : n + 1], (8, 256)))
        s = jnp.concatenate(scores, axis=0)
        m = jnp.max(s, axis=1, keepdims=True)
        e = jnp.exp(s - m)
        den = jnp.sum(e, axis=1, keepdims=True)
        w = e * jnp.concatenate(scale, axis=0)
        for n in range(16):
            part = w[n * 8 : n * 8 + 8].astype(BF16)
            out_ref[pl.ds(group * 128 + n * 8, 8), :128] = dot(part, buf[group, n, :, 128:], 1, 0)
        out_ref[pl.ds(group * 128, 128), 128:] = jnp.where(lane128 == 0, m, den)


def deal_kernel(turn_ref, p0, p1, p2, out_ref):
    rows = jnp.concatenate([p0[...], p1[...], p2[...]], axis=0)
    for r in range(4):
        out_ref[:, r * 256 : r * 256 + 256] = dot(rows, turn_ref[:, r * 256 : r * 256 + 256], 1, 0).astype(BF16)


def project_kernel(keep_ref, got_ref, turn_ref, early_ref, p3a, p3b, out_ref):
    zl = lax.axis_index("tensor") // 4
    weight = jnp.concatenate([keep_ref[...], got_ref[...]], axis=0)
    last = jnp.concatenate([p3a[...], p3b[...]], axis=0)
    for r in range(4):
        part = dot(last, turn_ref[:, r * 256 : r * 256 + 256], 1, 0).astype(BF16)
        rows = jnp.concatenate([early_ref[:, r * 256 : r * 256 + 256], part], axis=0)
        kv = dot(weight, rows, 1, 0).astype(BF16)
        out_ref[r * 2 + zl] = kv[:256]
        out_ref[r * 2 + 1 - zl] = kv[256:]


def total_of(ref):
    a = [ref[i].astype(F32) for i in range(8)]
    return ((a[0] + a[1]) + (a[2] + a[3])) + ((a[4] + a[5]) + (a[6] + a[7]))


def group_max(v):
    lane = lax.broadcasted_iota(jnp.int32, v.shape, 1)
    n = v.shape[1]
    for s in (1, 2, 4, 8):
        other = jnp.where((lane & s) == 0, pltpu.roll(v, n - s, 1), pltpu.roll(v, s, 1))
        v = jnp.maximum(v, other)
    return v


def quantize(kv):
    largest = group_max(jnp.max(jnp.abs(kv), axis=0, keepdims=True))
    scale = (largest + 1e-6) / 127.0
    return (kv / scale).astype(BF16), scale


def quantize_kernel(sum_ref, window_ref, *outs):
    kv = total_of(sum_ref)
    key_codes, key_scale = quantize(kv[:128])
    value_codes, value_scale = quantize(kv[128:])
    scales = pack_rows(three(key_scale) + three(value_scale), 16).astype(BF16)
    codes = jnp.concatenate([key_codes, value_codes, scales], axis=0)
    for d in range(4):
        outs[d][...] = dot(codes, window_ref[d], 1, 0).astype(BF16)


def join(steps, target_ref, q_ref, parts, tmp, acc, top, den):
    batch = lax.axis_index("batch")
    zh, core = batch // 2, lax.rem(batch, 2)
    q = q_ref[...]
    request = lax.broadcasted_iota(jnp.int32, (384, 128), 0) >> 3
    scales, highest = [], jnp.broadcast_to(top, (384, 128))
    for i, part in enumerate(parts):
        half = len(steps)
        origin = lax.rem(zh + 4 - steps[i % half], 4) * 2 + (core if i < half else 1 - core)
        rows = part[pl.ds(256, 16), :].astype(F32)
        key_scale = (rows[0:1] + rows[1:2]) + rows[2:3]
        scales.append((rows[3:4] + rows[4:5]) + rows[5:6])
        s = dot(q, part[pl.ds(0, 128), :], 1, 0) * (key_scale * (128.0**-0.5))
        s = jnp.where(request == target_ref[pl.ds(origin, 1), :], s, -jnp.inf)
        tmp[i] = s
        highest = jnp.maximum(highest, s)
    highest = jnp.max(highest, axis=1, keepdims=True)
    share = jnp.exp(top - highest)
    acc, total = acc * share, jnp.zeros((384, 128), F32)
    for i, part in enumerate(parts):
        e = jnp.exp(tmp[i] - highest)
        total = total + e
        acc = acc + dot((e * scales[i]).astype(BF16), part[pl.ds(128, 128), :], 1, 1)
    return acc, highest, den * share + jnp.sum(total, axis=1, keepdims=True)


def first_kernel(target_ref, q_ref, *refs):
    parts, (acc_ref, stat_ref, tmp) = refs[:6], refs[6:]
    low = jnp.full((384, 1), LOW, F32)
    acc, top, den = join((0, 1, 2), target_ref, q_ref, parts, tmp, jnp.zeros((384, 128), F32), low, jnp.zeros((384, 1), F32))
    acc_ref[...] = acc
    stat_ref[...] = pack_columns((top, den))


def last_kernel(target_ref, q_ref, acc_ref, stat_ref, own_ref, oth_ref, out_ref, tmp):
    top, den = stat_ref[:, 0:1], stat_ref[:, 1:2]
    acc, top, den = join((3,), target_ref, q_ref, (own_ref, oth_ref), tmp, acc_ref[...], top, den)
    out_ref[pl.ds(0, 128), :] = jnp.transpose(acc).astype(BF16)
    stats = pack_columns(three(top) + three(den))
    out_ref[pl.ds(128, 16), :] = jnp.transpose(stats)[:16].astype(BF16)


def final_kernel(u0, u1, u2, u3, r, out_ref, tmp):
    us = (u0, u1, u2, u3)
    tops, dens = [], []
    for u in us:
        rows = [u[pl.ds(128, 16), :].astype(F32)[i : i + 1] for i in range(6)]
        tops.append((rows[0] + rows[1]) + rows[2])
        dens.append((rows[3] + rows[4]) + rows[5])
    top = jnp.maximum(jnp.maximum(tops[0], tops[1]), jnp.maximum(tops[2], tops[3]))
    acc = jnp.zeros((128, 384), F32)
    den = jnp.zeros((1, 384), F32)
    for u, m, d in zip(us, tops, dens):
        share = jnp.exp(m - top)
        acc = acc + u[pl.ds(0, 128), :].astype(F32) * share
        den = den + d * share
    acc = jnp.transpose(acc)
    columns = jnp.transpose(pack_rows((top, den), 128))
    new_top, new_den = columns[:, 0:1], columns[:, 1:2]
    old_top, old_den = r[:, 128:129], r[:, 129:130]
    best = jnp.maximum(new_top, old_top)
    new_share, old_share = jnp.exp(new_top - best), jnp.exp(old_top - best)
    total = new_den * new_share + old_den * old_share
    tmp[...] = (acc * new_share + r[:, :128] * old_share) / total
    for q in range(8):
        out_ref[:, q * 128 : q * 128 + 128] = tmp[pl.ds(q, 48, stride=8), :].astype(BF16)


def shape(*dims, dtype=BF16):
    return jax.ShapeDtypeStruct(dims, dtype)


def role_shift(v, d):
    return lax.ppermute(v, "role", [(i, (i + d) % 4) for i in range(4)])


def x_shift(v, d):
    return lax.ppermute(v, "tensor", [(z * 4 + x, z * 4 + (x + d) % 4) for z in range(2) for x in range(4)])


def z_swap(v):
    return lax.ppermute(v, "tensor", [(t, (t + 4) % 8) for t in range(8)])


def zh_shift(v, d):
    return lax.ppermute(v, "batch", [(i, (i + 2 * d) % 8) for i in range(8)])


def core_swap(v):
    return lax.ppermute(v, "batch", [(i, i ^ 1) for i in range(8)])


def body(span, weight, queries, codes, scales, clen, bdest, brow):
    p0 = span.T
    p1, p2 = x_shift(p0, 1), x_shift(p0, -1)

    rows = weight.shape[0]
    keep, give, held = call(
        weight_kernel, [shape(256, rows // 2)] * 2 + [shape(*p0.shape)], (weight.reshape(rows, 256), p0), [FETCH] * 2,
        scratch=[pltpu.VMEM((rows // 2, 256), F32)],
    )
    got = z_swap(give)

    turn, window, target = call(
        plan_kernel, [shape(1024, 1024), shape(4, 256, 128), shape(8, 128, dtype=jnp.int32)],
        (bdest.T, brow.reshape(1, 512)), [FETCH] * 2, scratch=[pltpu.VMEM((512, 128), F32)], cost=2,
    )
    (p1, p2), target = lax.optimization_barrier(((p1, p2), target))

    cutoff = p0.shape[0] // 2
    p3a, p3b = x_shift(p1[:cutoff], 1), x_shift(p2[cutoff:], -1)

    count = p0.shape[1] // 4
    early = call(deal_kernel, shape(3 * p0.shape[0], p0.shape[1]), (turn, held, p1, p2), [VMEM] * 4, cost=1.5)
    outs = call(project_kernel, shape(8, 256, count), (keep, got, turn, early, p3a, p3b), [VMEM] * 6)
    groups = [[r * 8 + z * 4 + x for r in range(4) for z in range(2)] for x in range(4)]
    sums = lax.all_to_all(outs, ("role", "tensor"), 0, 0, axis_index_groups=groups)
    cuts = call(quantize_kernel, [shape(272, 128)] * 4, (sums, window), [VMEM] * 2)

    parts = [cuts[0]] + [zh_shift(cuts[d], d) for d in (1, 2, 3)]
    swapped = [core_swap(v) for v in parts]
    flat = queries.reshape(384, 128)
    so_far = call(
        first_kernel, [shape(384, 128, dtype=F32)] * 2, (target, flat, *parts[:3], *swapped[:3]), [VMEM] * 8,
        scratch=[pltpu.VMEM((6, 384, 128), F32)], cost=1,
    )
    sums = call(
        last_kernel, shape(144, 384), (target, flat, *so_far, parts[3], swapped[3]), [VMEM] * 6,
        scratch=[pltpu.VMEM((2, 384, 128), F32)], cost=0.7,
    )
    sums = [sums] + [role_shift(sums, d) for d in (1, 2, 3)]
    res = call(
        resident_kernel, shape(384, 256, dtype=F32), (clen, flat, jnp.swapaxes(scales, 3, 4).reshape(48, 2, 16), codes),
        [SMEM, VMEM, VMEM, ANY], scratch=[pltpu.VMEM((3, 16, 256, 256), BF16), pltpu.SemaphoreType.DMA((3,))], cost=5,
    )
    out = call(final_kernel, shape(48, 1024), (*sums, res), [VMEM] * 5, scratch=[pltpu.VMEM((384, 128), F32)])
    return out.reshape(3, 16, 1024)


def solution(mesh):
    return jax.shard_map(
        body,
        mesh=mesh,
        in_specs=(
            P("batch", ("role", "tensor")),
            P("role", "tensor", None),
            P(None, "batch", "tensor", None),
            P(None, "batch", "tensor", None, None),
            P(None, "batch", "tensor", None, None),
            P(None, "batch"),
            P(),
            P(),
        ),
        out_specs=P(None, "batch", "tensor"),
        check_vma=False,
    )
```

```python
import jax
import jax.numpy as jnp
from jax import lax
from jax.experimental import pallas as pl
from jax.experimental.pallas import tpu as pltpu
from jax.sharding import PartitionSpec as P

BLOCK = 16
LOW = -1e38
STEPS = (0, 3, 1, 2)
F32 = jnp.float32
BF16 = jnp.bfloat16
VMEM = pl.BlockSpec(memory_space=pltpu.VMEM)
FETCH = pl.BlockSpec()
SMEM = pl.BlockSpec(memory_space=pltpu.SMEM)
ANY = pl.BlockSpec(memory_space=pl.ANY)
def call(kernel, outs, args, specs, scratch=(), cost=1.0):
    return pl.pallas_call(
        kernel,
        out_shape=outs,
        in_specs=specs,
        out_specs=jax.tree.map(lambda _: VMEM, outs),
        scratch_shapes=list(scratch),
        compiler_params=pltpu.CompilerParams(vmem_limit_bytes=48 * 1024 * 1024),
        cost_estimate=pl.CostEstimate(flops=0, bytes_accessed=int(cost * 3_000_000), transcendentals=0),
    )(*args)


def dot(a, b, ca, cb):
    return lax.dot_general(a, b, (((ca,), (cb,)), ((), ())), preferred_element_type=F32)


def three(v):
    hi = v.astype(BF16).astype(F32)
    mid = (v - hi).astype(BF16).astype(F32)
    return hi, mid, v - hi - mid


def pack_columns(columns):
    lane = lax.broadcasted_iota(jnp.int32, (columns[0].shape[0], 128), 1)
    out = jnp.zeros(lane.shape, F32)
    for i, c in enumerate(columns):
        out = jnp.where(lane == i, c, out)
    return out


def pack_rows(rows, height):
    sub = lax.broadcasted_iota(jnp.int32, (height, rows[0].shape[1]), 0)
    out = jnp.zeros(sub.shape, F32)
    for i, c in enumerate(rows):
        out = jnp.where(sub == i, c, out)
    return out


def weight_kernel(w_ref, x_ref, keep_ref, give_ref, p_ref, tmp):
    p_ref[...] = x_ref[...]
    tensor = lax.axis_index("tensor")
    zl, x = tensor // 4, lax.rem(tensor, 4)
    rows = w_ref.shape[0] // 8
    for b, out_ref in enumerate((keep_ref, give_ref)):
        for s in range(4):
            start = (lax.rem(zl + b, 2) * 4 + lax.rem(x + STEPS[s], 4)) * rows
            tmp[pl.ds(s * rows, rows), :] = w_ref[pl.ds(pl.multiple_of(start, rows), rows), :].astype(F32)
        out_ref[pl.ds(0, 128), :] = jnp.transpose(tmp[:, :128]).astype(BF16)
        out_ref[pl.ds(128, 128), :] = jnp.transpose(tmp[:, 128:]).astype(BF16)


def plan_kernel(dest_ref, row_ref, turn_ref, window_ref, target_ref, tmp):
    batch, role = lax.axis_index("batch"), lax.axis_index("role")
    zh = batch // 2
    dest = dest_ref[...]
    key = (dest & 7) >> 1
    index = lax.broadcasted_iota(jnp.int32, (1, 512), 1)
    key_i, order_i = key.astype(F32), (key * 512 + index).astype(F32)
    columns = jnp.transpose(pack_rows((key_i, order_i), 128))
    key_j, order_j = columns[:, 0:1], columns[:, 1:2]
    one = lax.broadcasted_iota(jnp.int32, (512, 512), 0)
    two = lax.broadcasted_iota(jnp.int32, (512, 512), 1)
    same = (one >> 6) == (two >> 6)
    rank = jnp.sum(jnp.where(same & (order_i < order_j), 1.0, 0.0), axis=1, keepdims=True).astype(jnp.int32)
    less = jnp.sum(jnp.where(same & (key_i < key_j), 1.0, 0.0), axis=1, keepdims=True).astype(jnp.int32)
    owner, slot = rank & 3, rank >> 2
    place = slot - ((less - owner + 3) >> 2)
    lane = lax.broadcasted_iota(jnp.int32, (512, 128), 1) >> 4
    pick = jnp.where((owner == role) & (place == lane), 1.0, 0.0).astype(BF16)
    request = jnp.where((dest & 7) == batch, (dest >> 3) * 16 + row_ref[...] + 1, 0)
    sub = lax.broadcasted_iota(jnp.int32, (8, 512), 0)
    spread = jnp.where((lax.broadcasted_iota(jnp.int32, (8, 512), 1) >> 6) == sub, request, 0)
    target_ref[...] = dot(spread.astype(F32).astype(BF16), pick, 1, 0).astype(jnp.int32) - 1
    gap = lax.broadcasted_iota(jnp.int32, (256, 128), 0) - lax.broadcasted_iota(jnp.int32, (256, 128), 1)
    for d in range(4):
        before = ((index >> 6) == batch) & (key < lax.rem(zh + d, 4))
        count = jnp.sum(jnp.where(before, 1.0, 0.0), axis=1, keepdims=True).astype(jnp.int32)
        window_ref[d] = jnp.where(gap == ((count - role + 3) >> 2) * 16, 1.0, 0.0).astype(BF16)
    tmp[...] = jnp.broadcast_to((owner * 16 + slot).astype(F32), (512, 128))
    own = tmp[pl.ds(pl.multiple_of(batch * 64, 64), 64), :].astype(BF16)
    token = lax.broadcasted_iota(jnp.int32, (1024, 64), 0)
    repeat = jnp.where((token >> 4) == lax.broadcasted_iota(jnp.int32, (1024, 64), 1), 1.0, 0.0).astype(BF16)
    to = dot(repeat, own, 1, 0).astype(jnp.int32)[:, 0:1] * 16 + (token[:, 0:1] & 15)
    turn_ref[...] = jnp.where(lax.broadcasted_iota(jnp.int32, (1024, 1024), 1) == to, 1.0, 0.0).astype(BF16)


def resident_kernel(len_ref, q_ref, sc_ref, c_ref, out_ref, buf, sems):
    copies = [
        pltpu.make_async_copy(c_ref.at[i, :, 0], buf.at[i], sems.at[i])
        for i in range(3)
    ]
    for c in copies:
        c.start()
    lane = lax.broadcasted_iota(jnp.int32, (8, 256), 1)
    lane128 = lax.broadcasted_iota(jnp.int32, (128, 128), 1)
    column = lax.broadcasted_iota(jnp.int32, (16, 256), 0)
    block = lax.broadcasted_iota(jnp.int32, (16, 256), 1) >> 4
    pick = jnp.where(column == block, 1.0, 0.0).astype(BF16)
    for group in range(3):
        spread = []
        for half in range(2):
            parts = [p.astype(BF16) for p in three(sc_ref[pl.ds(group * 16, 16), half, :])]
            spread.append((dot(parts[0], pick, 1, 0) + dot(parts[1], pick, 1, 0)) + dot(parts[2], pick, 1, 0))
        ks, vs = spread[0] * (128.0**-0.5), spread[1]
        turned = jnp.transpose(q_ref[pl.ds(group * 128, 128), :].astype(F32))
        copies[group].wait()
        s = jnp.zeros((256, 128), F32)
        for n in range(0, 16, 2):
            keys = jnp.concatenate([buf[group, n, :, :128], buf[group, n + 1, :, :128]], axis=1)
            own = [jnp.where((lane128 >> 3) == n + i, turned, 0.0).astype(BF16) for i in range(2)]
            s = s + dot(keys, jnp.concatenate(own, axis=0), 1, 0)
        s = jnp.transpose(s)
        scores, scale = [], []
        for n in range(16):
            live = lane < len_ref[group, n]
            scores.append(jnp.where(live, s[n * 8 : n * 8 + 8] * ks[n : n + 1], -jnp.inf))
            scale.append(jnp.broadcast_to(vs[n : n + 1], (8, 256)))
        s = jnp.concatenate(scores, axis=0)
        m = jnp.max(s, axis=1, keepdims=True)
        e = jnp.exp(s - m)
        den = jnp.sum(e, axis=1, keepdims=True)
        w = e * jnp.concatenate(scale, axis=0)
        for n in range(16):
            part = w[n * 8 : n * 8 + 8].astype(BF16)
            out_ref[pl.ds(group * 128 + n * 8, 8), :128] = dot(part, buf[group, n, :, 128:], 1, 0)
        out_ref[pl.ds(group * 128, 128), 128:] = jnp.where(lane128 == 0, m, den)


def deal_kernel(turn_ref, p0, p1, p2, out_ref):
    rows = jnp.concatenate([p0[...], p1[...], p2[...]], axis=0)
    for r in range(4):
        out_ref[:, r * 256 : r * 256 + 256] = dot(rows, turn_ref[:, r * 256 : r * 256 + 256], 1, 0).astype(BF16)


def project_kernel(keep_ref, got_ref, turn_ref, early_ref, p3a, p3b, out_ref):
    zl = lax.axis_index("tensor") // 4
    weight = jnp.concatenate([keep_ref[...], got_ref[...]], axis=0)
    last = jnp.concatenate([p3a[...], p3b[...]], axis=0)
    for r in range(4):
        part = dot(last, turn_ref[:, r * 256 : r * 256 + 256], 1, 0).astype(BF16)
        rows = jnp.concatenate([early_ref[:, r * 256 : r * 256 + 256], part], axis=0)
        kv = dot(weight, rows, 1, 0).astype(BF16)
        out_ref[r * 2 + zl] = kv[:256]
        out_ref[r * 2 + 1 - zl] = kv[256:]


def total_of(ref):
    a = [ref[i].astype(F32) for i in range(8)]
    return ((a[0] + a[1]) + (a[2] + a[3])) + ((a[4] + a[5]) + (a[6] + a[7]))


def group_max(v):
    lane = lax.broadcasted_iota(jnp.int32, v.shape, 1)
    n = v.shape[1]
    for s in (1, 2, 4, 8):
        other = jnp.where((lane & s) == 0, pltpu.roll(v, n - s, 1), pltpu.roll(v, s, 1))
        v = jnp.maximum(v, other)
    return v


def quantize(kv):
    largest = group_max(jnp.max(jnp.abs(kv), axis=0, keepdims=True))
    scale = (largest + 1e-6) / 127.0
    return (kv / scale).astype(BF16), scale


def quantize_kernel(sum_ref, window_ref, *outs):
    kv = total_of(sum_ref)
    key_codes, key_scale = quantize(kv[:128])
    value_codes, value_scale = quantize(kv[128:])
    scales = pack_rows(three(key_scale) + three(value_scale), 16).astype(BF16)
    codes = jnp.concatenate([key_codes, value_codes, scales], axis=0)
    for d in range(4):
        outs[d][...] = dot(codes, window_ref[d], 1, 0).astype(BF16)


def join(steps, target_ref, q_ref, parts, tmp, acc, top, den):
    batch = lax.axis_index("batch")
    zh, core = batch // 2, lax.rem(batch, 2)
    q = q_ref[...]
    request = lax.broadcasted_iota(jnp.int32, (384, 128), 0) >> 3
    scales, highest = [], jnp.broadcast_to(top, (384, 128))
    for i, part in enumerate(parts):
        half = len(steps)
        origin = lax.rem(zh + 4 - steps[i % half], 4) * 2 + (core if i < half else 1 - core)
        rows = part[pl.ds(256, 16), :].astype(F32)
        key_scale = (rows[0:1] + rows[1:2]) + rows[2:3]
        scales.append((rows[3:4] + rows[4:5]) + rows[5:6])
        s = dot(q, part[pl.ds(0, 128), :], 1, 0) * (key_scale * (128.0**-0.5))
        s = jnp.where(request == target_ref[pl.ds(origin, 1), :], s, -jnp.inf)
        tmp[i] = s
        highest = jnp.maximum(highest, s)
    highest = jnp.max(highest, axis=1, keepdims=True)
    share = jnp.exp(top - highest)
    acc, total = acc * share, jnp.zeros((384, 128), F32)
    for i, part in enumerate(parts):
        e = jnp.exp(tmp[i] - highest)
        total = total + e
        acc = acc + dot((e * scales[i]).astype(BF16), part[pl.ds(128, 128), :], 1, 1)
    return acc, highest, den * share + jnp.sum(total, axis=1, keepdims=True)


def first_kernel(target_ref, q_ref, *refs):
    parts, (acc_ref, stat_ref, tmp) = refs[:6], refs[6:]
    low = jnp.full((384, 1), LOW, F32)
    acc, top, den = join((0, 1, 2), target_ref, q_ref, parts, tmp, jnp.zeros((384, 128), F32), low, jnp.zeros((384, 1), F32))
    acc_ref[...] = acc
    stat_ref[...] = pack_columns((top, den))


def last_kernel(target_ref, q_ref, acc_ref, stat_ref, own_ref, oth_ref, out_ref, tmp):
    top, den = stat_ref[:, 0:1], stat_ref[:, 1:2]
    acc, top, den = join((3,), target_ref, q_ref, (own_ref, oth_ref), tmp, acc_ref[...], top, den)
    out_ref[pl.ds(0, 128), :] = jnp.transpose(acc).astype(BF16)
    rows = jnp.transpose(pack_columns((top, den)))
    out_ref[pl.ds(128, 16), :] = pack_rows(three(rows[0:1]) + three(rows[1:2]), 16).astype(BF16)


def final_kernel(u0, u1, u2, u3, r, out_ref, tmp):
    us = (u0, u1, u2, u3)
    tops, dens = [], []
    for u in us:
        rows = [u[pl.ds(128, 16), :].astype(F32)[i : i + 1] for i in range(6)]
        tops.append((rows[0] + rows[1]) + rows[2])
        dens.append((rows[3] + rows[4]) + rows[5])
    top = jnp.maximum(jnp.maximum(tops[0], tops[1]), jnp.maximum(tops[2], tops[3]))
    acc = jnp.zeros((128, 384), F32)
    den = jnp.zeros((1, 384), F32)
    for u, m, d in zip(us, tops, dens):
        share = jnp.exp(m - top)
        acc = acc + u[pl.ds(0, 128), :].astype(F32) * share
        den = den + d * share
    acc = jnp.transpose(acc)
    columns = jnp.transpose(pack_rows((top, den), 128))
    new_top, new_den = columns[:, 0:1], columns[:, 1:2]
    old_top, old_den = r[:, 128:129], r[:, 129:130]
    best = jnp.maximum(new_top, old_top)
    new_share, old_share = jnp.exp(new_top - best), jnp.exp(old_top - best)
    total = new_den * new_share + old_den * old_share
    tmp[...] = (acc * new_share + r[:, :128] * old_share) / total
    for q in range(8):
        out_ref[:, q * 128 : q * 128 + 128] = tmp[pl.ds(q, 48, stride=8), :].astype(BF16)


def shape(*dims, dtype=BF16):
    return jax.ShapeDtypeStruct(dims, dtype)


def role_shift(v, d):
    return lax.ppermute(v, "role", [(i, (i + d) % 4) for i in range(4)])


def x_shift(v, d):
    return lax.ppermute(v, "tensor", [(z * 4 + x, z * 4 + (x + d) % 4) for z in range(2) for x in range(4)])


def z_swap(v):
    return lax.ppermute(v, "tensor", [(t, (t + 4) % 8) for t in range(8)])


def zh_shift(v, d):
    return lax.ppermute(v, "batch", [(i, (i + 2 * d) % 8) for i in range(8)])


def core_swap(v):
    return lax.ppermute(v, "batch", [(i, i ^ 1) for i in range(8)])


def body(span, weight, queries, codes, scales, clen, bdest, brow):
    p0 = span.T
    p1, p2 = x_shift(p0, 1), x_shift(p0, -1)

    rows = weight.shape[0]
    keep, give, held = call(
        weight_kernel, [shape(256, rows // 2)] * 2 + [shape(*p0.shape)], (weight.reshape(rows, 256), p0), [FETCH] * 2,
        scratch=[pltpu.VMEM((rows // 2, 256), F32)],
    )
    got = z_swap(give)

    turn, window, target = call(
        plan_kernel, [shape(1024, 1024), shape(4, 256, 128), shape(8, 128, dtype=jnp.int32)],
        (bdest.T, brow.reshape(1, 512)), [FETCH] * 2, scratch=[pltpu.VMEM((512, 128), F32)], cost=2,
    )
    (p1, p2), target = lax.optimization_barrier(((p1, p2), target))

    cutoff = p0.shape[0] // 2
    p3a, p3b = x_shift(p1[:cutoff], 1), x_shift(p2[cutoff:], -1)

    count = p0.shape[1] // 4
    early = call(deal_kernel, shape(3 * p0.shape[0], p0.shape[1]), (turn, held, p1, p2), [VMEM] * 4, cost=1.5)
    outs = call(project_kernel, shape(8, 256, count), (keep, got, turn, early, p3a, p3b), [VMEM] * 6)
    groups = [[r * 8 + z * 4 + x for r in range(4) for z in range(2)] for x in range(4)]
    sums = lax.all_to_all(outs, ("role", "tensor"), 0, 0, axis_index_groups=groups)
    cuts = call(quantize_kernel, [shape(272, 128)] * 4, (sums, window), [VMEM] * 2)

    parts = [cuts[0]] + [zh_shift(cuts[d], d) for d in (1, 2, 3)]
    swapped = [core_swap(v) for v in parts]
    flat = queries.reshape(384, 128)
    so_far = call(
        first_kernel, [shape(384, 128, dtype=F32)] * 2, (target, flat, *parts[:3], *swapped[:3]), [VMEM] * 8,
        scratch=[pltpu.VMEM((6, 384, 128), F32)], cost=1,
    )
    sums = call(
        last_kernel, shape(144, 384), (target, flat, *so_far, parts[3], swapped[3]), [VMEM] * 6,
        scratch=[pltpu.VMEM((2, 384, 128), F32)], cost=0.7,
    )
    sums = [sums] + [role_shift(sums, d) for d in (1, 2, 3)]
    res = call(
        resident_kernel, shape(384, 256, dtype=F32), (clen, flat, jnp.swapaxes(scales, 3, 4).reshape(48, 2, 16), codes),
        [SMEM, VMEM, VMEM, ANY], scratch=[pltpu.VMEM((3, 16, 256, 256), BF16), pltpu.SemaphoreType.DMA((3,))], cost=5,
    )
    out = call(final_kernel, shape(48, 1024), (*sums, res), [VMEM] * 5, scratch=[pltpu.VMEM((384, 128), F32)])
    return out.reshape(3, 16, 1024)


def solution(mesh):
    return jax.shard_map(
        body,
        mesh=mesh,
        in_specs=(
            P("batch", ("role", "tensor")),
            P("role", "tensor", None),
            P(None, "batch", "tensor", None),
            P(None, "batch", "tensor", None, None),
            P(None, "batch", "tensor", None, None),
            P(None, "batch"),
            P(),
            P(),
        ),
        out_specs=P(None, "batch", "tensor"),
        check_vma=False,
    )
```
